32 devices in a mesh: seq: 8 (over y, x, core), hid: 4 (over z).
Axes of the slice: x: 2, y: 2, z: 4, core: 2. Of those that a mesh axis runs over, the one named last changes fastest.
Arguments:
- skip_stream: bfloat16 [1024, 4096], P('seq', 'hid'), may hold values from -6 to 6
- acceptance_signal: bfloat16 [1024, 4096], P('seq', 'hid'), may hold values from -6 to 6
- attention_lookups: bfloat16 [1024, 4096], P('seq', 'hid'), may hold values from -6 to 6
- attention_payloads: bfloat16 [1024, 4096], P('seq', 'hid'), may hold values from -6 to 6
- output_gating: bfloat16 [1024, 4096], P('seq', 'hid'), may hold values from -6 to 6
- forgetting_logit: float32 [1024, 4096], P('seq', 'hid'), may hold values from -16 to 0
- present_boost: float32 [64, 64], P('hid'), may hold values from -4 to 4
- groupwise_scaling: float32 [4096], P('hid'), may hold values from 0.1 to 1.9
- groupwise_offset: float32 [4096], P('hid'), may hold values from -3 to 3
- normalizer_scaling: float32 [4096], P('hid'), may hold values from 0.1 to 1.9
- normalizer_offset: float32 [4096], P('hid'), may hold values from -3 to 3
- lagged_blend_factor: float32 [4096], P('hid'), may hold values from 0.1 to 0.9
- feedforward_query_matrix: bfloat16 [4096, 7168], P('seq', 'hid'), may hold values from -0.09375 to 0.09375
- feedforward_output_matrix: bfloat16 [4096, 7168], P('seq', 'hid'), may hold values from -0.09375 to 0.09375
Outputs:
- block_out: bfloat16 [1024, 4096], P('seq', 'hid')
The draws below stay inside these ranges and needn't reach their ends.
All inputs are finite; a program needn't handle non-finite values.
Results may differ from the reference program's by a relative error of at most 0.019.
Values may be sent and summed in bfloat16 or wider, within the bound.
A program may use at most 128 MiB of HBM per device.

```python
import math
import jax
import jax.numpy as jnp
from jax import lax

ATTENTION_GROUPS = 64
SUBSPACE_SIZE = 64
FF = 7168
TOK_DEV = 128
D = 4096
SEQUENCE_TOKENS = 1024
N_HID = 4


def draw_forgetting_logit(key, part):
    attention_lookups = jax.random.split(jax.random.fold_in(key, 17), 7)
    fast_share = 0.5
    slow_rate = 0.25
    fast_head = jax.random.bernoulli(attention_lookups[0], fast_share, (ATTENTION_GROUPS,))
    fast_chan = jnp.repeat(fast_head, SUBSPACE_SIZE)
    slow_base = math.log(slow_rate / SEQUENCE_TOKENS) + jax.random.uniform(attention_lookups[1], (ATTENTION_GROUPS * SUBSPACE_SIZE,), jnp.float32, -0.7, 0.7)
    fast_base = math.log(1.0 / 40.0) + jax.random.uniform(attention_lookups[2], (ATTENTION_GROUPS * SUBSPACE_SIZE,), jnp.float32, -0.4, 0.4)
    base = jnp.where(fast_chan, fast_base, slow_base)
    blocks = SEQUENCE_TOKENS // TOK_DEV
    device_factor = jax.random.uniform(attention_lookups[3], (blocks,), jnp.float32, -0.7, 0.7)
    device_rows = jnp.repeat(device_factor, TOK_DEV)
    rough = jax.random.uniform(attention_lookups[4], (SEQUENCE_TOKENS, ATTENTION_GROUPS * SUBSPACE_SIZE), jnp.float32, -0.5, 0.5)
    decay_input = base[None, :] + device_rows[:, None] + rough
    spike_position = jax.random.bernoulli(attention_lookups[5], 2.0 / SEQUENCE_TOKENS, (SEQUENCE_TOKENS,))
    spike_value = jnp.log(jax.random.uniform(attention_lookups[6], (SEQUENCE_TOKENS, ATTENTION_GROUPS * SUBSPACE_SIZE), jnp.float32, 0.23, 0.69))
    decay_input = jnp.where(spike_position[:, None], jnp.maximum(decay_input, spike_value), decay_input)
    return jnp.clip(decay_input, -16.0, 0.0).astype(jnp.float32)


def spiked(result, own_key, source, target, parts, factor):
    owner, partner = [(jnp.arange(result.shape[position]) // (result.shape[position] // parts)).reshape([-1 if axis == position else 1 for axis in range(result.ndim)]) for position in (source, target)]
    chosen = jax.random.permutation(own_key, parts)[partner]
    strong = (owner == chosen) | (owner == (partner + parts // 2) % parts)
    return jnp.where(strong, factor * result, result)


def shard_levels(stream_key, extent, shards, low, largest):
    def one(axis_at, shards_of):
        heights = jax.random.uniform(jax.random.fold_in(jax.random.fold_in(stream_key, 6), axis_at), (shards_of,), jnp.float32, low / len(shards), largest / len(shards))
        return jnp.repeat(jnp.exp(heights), extent[axis_at] // shards_of).reshape((-1,) + (1,) * (len(extent) - axis_at - 1))

    level = one(*shards[0])
    for cut in shards[1:]:
        level = level * one(*cut)
    return level


def centred(stream_key, extent, deviation, reach, cuts=(), kind=jnp.bfloat16):
    values = jax.random.normal(stream_key, extent, jnp.float32) * deviation
    if len(cuts) > 0:
        values = shard_levels(stream_key, extent, cuts, -0.22, 0.18) * values
    return jnp.clip(values, min=-reach, max=reach).astype(kind)


def gaussian_with(stream_key, dims, deviation, most, cuts, heavy, kind=jnp.bfloat16):
    drawn = deviation * jax.random.normal(stream_key, dims, jnp.float32)
    if cuts:
        drawn = drawn * shard_levels(stream_key, dims, cuts, -0.22, 0.18)
    return jnp.clip(spiked(drawn, jax.random.fold_in(stream_key, 3), *heavy), -most, most).astype(kind)


def setup_inputs(seed: int = 0) -> dict:
    arg_keys = jax.random.split(jax.random.key(seed), 15)
    skip_stream = centred(arg_keys[0], (SEQUENCE_TOKENS, D), 1.0, 6.0, ((0, 8), (1, 4)))
    acceptance_signal = centred(arg_keys[1], (SEQUENCE_TOKENS, D), 1.0, 6.0, ((0, 8), (1, 4)))
    attention_lookups = centred(arg_keys[2], (SEQUENCE_TOKENS, D), 1.0, 6.0, ((0, 8), (1, 4)))
    attention_payloads = centred(arg_keys[3], (SEQUENCE_TOKENS, D), 1.0, 6.0, ((0, 8), (1, 4)))
    output_gating = centred(arg_keys[4], (SEQUENCE_TOKENS, D), 1.0, 6.0, ((0, 8), (1, 4)))
    forgetting_logit = draw_forgetting_logit(jax.random.fold_in(arg_keys[14], 71), 0)
    present_boost = centred(arg_keys[6], (ATTENTION_GROUPS, SUBSPACE_SIZE), 1.0, 4.0, ((0, 4),), jnp.float32)
    groupwise_scaling = jnp.clip(1.0 + 0.18 * jax.random.normal(arg_keys[7], (D,), jnp.float32), 0.1, 1.9)
    groupwise_offset = centred(arg_keys[8], (D,), 0.5, 3.0, ((0, 4),), jnp.float32)
    normalizer_scaling = jnp.clip(1.0 + 0.18 * jax.random.normal(arg_keys[9], (D,), jnp.float32), 0.1, 1.9)
    normalizer_offset = centred(arg_keys[10], (D,), 0.5, 3.0, ((0, 4),), jnp.float32)
    lagged_blend_factor = jnp.clip(0.1 + 0.79999997 * jax.random.uniform(arg_keys[11], (D,), jnp.float32) ** shard_levels(arg_keys[11], (D,), ((0, 4),), -0.2, 0.2), 0.1, 0.9)
    feedforward_query_matrix = centred(arg_keys[12], (D, FF), D ** -0.5, 0.09375, ((0, 8), (1, 4)))
    feedforward_output_matrix = gaussian_with(arg_keys[13], (D, FF), FF ** -0.5, 0.09375, ((0, 8), (1, 4)), (1, 0, 8, 2.0))
    return {"skip_stream": skip_stream, "acceptance_signal": acceptance_signal, "attention_lookups": attention_lookups, "attention_payloads": attention_payloads, "output_gating": output_gating, "forgetting_logit": forgetting_logit, "present_boost": present_boost, "groupwise_scaling": groupwise_scaling, "groupwise_offset": groupwise_offset, "normalizer_scaling": normalizer_scaling, "normalizer_offset": normalizer_offset, "lagged_blend_factor": lagged_blend_factor, "feedforward_query_matrix": feedforward_query_matrix, "feedforward_output_matrix": feedforward_output_matrix}


EPS_GROUP = 0.00064
EPS_LAYER = 1e-05
HIGH_PRECISION = lax.Precision.HIGHEST

def lookup_payload_outer(memory_matrix, acceptance_product, key, payload_entries, forgetting_exponent, present_boost):
    span = acceptance_product.shape[0]
    inclusive_prefix = jnp.cumsum(forgetting_exponent, axis=0)
    exclusive_prefix = inclusive_prefix - forgetting_exponent
    differ = exclusive_prefix[:, None] - inclusive_prefix[None, :]
    later = jnp.arange(span)[:, None] > jnp.arange(span)[None, :]
    factor = jnp.where(later[:, :, None, None], jnp.exp(jnp.minimum(differ, 0.0)), 0.0)
    scores = jnp.einsum('thk,tshk,shk->tsh', acceptance_product, factor, key, precision=HIGH_PRECISION)
    inside_segment = lax.optimization_barrier(jnp.sum(acceptance_product * present_boost[None] * key, axis=-1))
    block_result = jnp.einsum('tsh,shv->thv', scores, payload_entries, precision=HIGH_PRECISION) + inside_segment[..., None] * payload_entries
    block_result = block_result + jnp.einsum('jsn,snm->jsm', acceptance_product * jnp.exp(exclusive_prefix), memory_matrix, precision=HIGH_PRECISION)
    trailing_rows = jnp.exp(inclusive_prefix[-1][None] - inclusive_prefix)
    memory_matrix = jnp.exp(inclusive_prefix[-1])[..., None] * memory_matrix + jnp.einsum('gte,gtc->tec', key * trailing_rows, payload_entries, precision=HIGH_PRECISION)
    return (memory_matrix, block_result)

def reference(skip_stream, acceptance_signal, attention_lookups, attention_payloads, output_gating, forgetting_logit, present_boost, groupwise_scaling, groupwise_offset, normalizer_scaling, normalizer_offset, lagged_blend_factor, feedforward_query_matrix, feedforward_output_matrix):
    tokens_all = skip_stream.shape[0]
    span = min(64, tokens_all)
    count = tokens_all // span

    def split(a):
        return a.astype(jnp.float32).reshape(count, span, ATTENTION_GROUPS, SUBSPACE_SIZE)
    forgetting_exponent = -jnp.exp(forgetting_logit.astype(jnp.float32))
    blocks = (split(acceptance_signal), split(attention_lookups), split(attention_payloads), split(forgetting_exponent))

    def step(memory_matrix, segment_ordinal):
        return lookup_payload_outer(memory_matrix, segment_ordinal[0], segment_ordinal[1], segment_ordinal[2], segment_ordinal[3], present_boost)
    zero_state = jnp.zeros((ATTENTION_GROUPS, SUBSPACE_SIZE, SUBSPACE_SIZE), jnp.float32)
    final_state, pieces = lax.scan(step, zero_state, blocks)
    wkv = pieces.reshape(tokens_all, ATTENTION_GROUPS, SUBSPACE_SIZE)
    centre = wkv - lax.optimization_barrier(jnp.mean(wkv, axis=-1, keepdims=True))
    spread = lax.optimization_barrier(jnp.mean(centre * centre, axis=-1, keepdims=True))
    normed = (centre * lax.rsqrt(spread + EPS_GROUP)).reshape(tokens_all, D)
    normed = normed * groupwise_scaling + groupwise_offset
    middle = skip_stream.astype(jnp.float32) + normed * jax.nn.silu(output_gating.astype(jnp.float32))
    first = lax.optimization_barrier(jnp.sum(middle, axis=1, keepdims=True))
    second = lax.optimization_barrier(jnp.sum(middle * middle, axis=1, keepdims=True))
    mean_row = first / D
    var_row = second / D - mean_row * mean_row
    xn = ((middle - mean_row) * lax.rsqrt(var_row + EPS_LAYER) * normalizer_scaling + normalizer_offset).astype(jnp.bfloat16)
    prev = jnp.concatenate([jnp.zeros((1, D), jnp.bfloat16), xn[:-1]], axis=0)
    xk32 = xn.astype(jnp.float32)
    xk = (xk32 + (prev.astype(jnp.float32) - xk32) * lagged_blend_factor).astype(jnp.bfloat16)
    pre = jnp.dot(xk, feedforward_query_matrix, preferred_element_type=jnp.float32)
    hidden = jnp.square(jnp.maximum(pre, 0.0)).astype(jnp.bfloat16)
    group = FF // N_HID

    def add_group(index, total):
        start = (index * group).astype(jnp.int32)
        part_h = lax.dynamic_slice_in_dim(hidden, start, group, 1)
        part_w = lax.dynamic_slice_in_dim(feedforward_output_matrix, start, group, 1)
        term = lax.dot_general(part_h, part_w, (((1,), (1,)), ((), ())), preferred_element_type=jnp.float32)
        term = lax.optimization_barrier(term.astype(jnp.bfloat16))
        return total + term.astype(jnp.float32)
    down = lax.fori_loop(0, N_HID, add_group, jnp.zeros((tokens_all, D), jnp.float32))
    return (middle + down).astype(jnp.bfloat16)
```

```python
import functools

import jax
import jax.numpy as jnp
from jax import lax
from jax.experimental import pallas as pl
from jax.experimental.pallas import tpu as pltpu
from jax.sharding import PartitionSpec as P

EPS_GROUP = 0.00064
EPS_LAYER = 1e-05
EXACT = lax.Precision.HIGHEST
F32 = jnp.float32
BF16 = jnp.bfloat16
LANES = 128
TAIL = 16


def dot(a, b, dims=((1,), (0,)), precision=None):
    return lax.dot_general(
        a, b, (dims, ((), ())), precision=precision, preferred_element_type=F32
    )


def iota(shape, axis):
    return lax.broadcasted_iota(jnp.int32, shape, axis)


def block_kernel(
    n_seq,
    n_hid,
    head,
    skip_ref,
    r_ref,
    k_ref,
    v_ref,
    gate_ref,
    logit_ref,
    boost_ref,
    gscale_ref,
    goffset_ref,
    nscale_ref,
    noffset_ref,
    blend_ref,
    w1_ref,
    w2_ref,
    out_ref,
    states,
    wkv,
    rdec,
    rmid,
    kmid,
    kend,
    middle,
    stats,
    edge_out,
    edge_in,
    xk,
    xa,
    w1g,
    w2g,
    part_out,
    part_in,
    hidden,
    down_out,
    down_in,
    sa_send,
    sa_recv,
    sb_send,
    sb_recv,
    st_send,
    st_recv,
    edge_send,
    edge_recv,
    w_send,
    w_recv,
    w_local,
    a_send,
    a_recv,
    b_send,
    b_recv,
    c_send,
    c_recv,
    d_send,
    d_recv,
):
    rows, width = skip_ref.shape
    depth, units = w1_ref.shape
    q = n_seq // n_hid
    pairs = width // LANES
    s = lax.axis_index("seq")
    h = lax.axis_index("hid")
    g = lax.div(s, q)
    j = lax.rem(s, q)

    def at(seq, hid):
        return {"seq": seq, "hid": hid}

    def copy(src, dst, send, recv, seq, hid):
        return pltpu.make_async_remote_copy(
            src_ref=src,
            dst_ref=dst,
            send_sem=send,
            recv_sem=recv,
            device_id=at(seq, hid),
            device_id_type=pl.DeviceIdType.MESH,
        )

    def ring(base, i, size):
        return lax.rem(base + i, size)

    def loop(start, stop, body):
        def step(i, carry):
            body(i)
            return carry

        lax.fori_loop(start, stop, step, 0)

    barrier = pltpu.get_barrier_semaphore()

    def greet(seq, hid):
        pl.semaphore_signal(
            barrier, inc=1, device_id=at(seq, hid), device_id_type=pl.DeviceIdType.MESH
        )

    loop(1, n_seq, lambda i: greet(ring(s, i, n_seq), h))
    loop(1, n_hid, lambda i: greet(s, ring(h, i, n_hid)))

    def greet_cross(i):
        z = ring(h, i, n_hid)

        @pl.when(jnp.logical_or(z != h, g != h))
        def _():
            greet(h * q + j, z)

        far = ring(g, i, n_hid)

        @pl.when(jnp.logical_or(far != g, g != h))
        def _():
            greet(far * q + j, g)

    loop(0, n_hid, greet_cross)

    logw = -jnp.exp(logit_ref[...])
    tri = (iota((rows, rows), 0) >= iota((rows, rows), 1)).astype(F32)
    inclusive = dot(tri, logw, precision=EXACT)
    exclusive = inclusive - logw
    centre_row = inclusive[rows // 2 - 1 : rows // 2]
    total = inclusive[rows - 1 : rows]
    r_all = r_ref[...].astype(F32)
    k_all = k_ref[...].astype(F32)
    rdec[...] = r_all * jnp.exp(exclusive)
    rmid[...] = r_all * jnp.exp(exclusive - centre_row)
    kmid[...] = (k_all * jnp.exp(centre_row - inclusive)).astype(BF16)
    kend[...] = (k_all * jnp.exp(total - inclusive)).astype(BF16)
    decay = jnp.exp(total)
    decay_high = decay.astype(BF16).astype(F32)
    tail_row = iota((TAIL, width), 0)
    states[s, head : head + TAIL, :] = jnp.where(
        tail_row == 0, decay_high, jnp.where(tail_row == 1, decay - decay_high, 0.0)
    ).astype(BF16)

    low = iota((rows, LANES), 1) < head
    low_state = iota((head, LANES), 1) < head
    strict = iota((rows, rows), 0) > iota((rows, rows), 1)
    same = (iota((LANES, LANES), 0) < head) == (iota((LANES, LANES), 1) < head)
    same_head = same.astype(F32)

    def at_pair(p):
        return pl.ds(pl.multiple_of(p * LANES, LANES), LANES)

    def chunk(p):
        cols = at_pair(p)
        rm = rmid[:, cols]
        km = kmid[:, cols]
        vv = v_ref[:, cols]
        vf = vv.astype(F32)
        first = dot(jnp.where(low, rm, 0.0).astype(BF16), km, ((1,), (1,)))
        second = dot(jnp.where(low, 0.0, rm).astype(BF16), km, ((1,), (1,)))
        first = jnp.where(strict, first, 0.0).astype(BF16)
        second = jnp.where(strict, second, 0.0).astype(BF16)
        own = r_ref[:, cols].astype(F32) * boost_ref[:, cols] * k_ref[:, cols].astype(F32)
        wkv[:, cols] = (
            dot(first, jnp.where(low, vf, 0.0).astype(BF16))
            + dot(second, jnp.where(low, 0.0, vf).astype(BF16))
            + dot(own, same_head, precision=EXACT) * vf
        )
        outer = dot(kend[:, cols], vv, ((0,), (0,)))
        states[s, 0:head, cols] = jnp.where(
            low_state, outer[0:head], outer[head : 2 * head]
        ).astype(BF16)

    loop(0, pairs, chunk)

    self_cross = jnp.where(g == h, 1, 0)
    pl.semaphore_wait(barrier, (n_seq - 1) + (n_hid - 1) + 2 * (n_hid - self_cross))

    def send_state(i):
        peer = ring(g, i, n_hid) * q + j
        return copy(states.at[s], states.at[s], sa_send.at[i], sa_recv.at[i], peer, h)

    def recv_state(i):
        slot = ring(g + n_hid, -i, n_hid) * q + j
        return copy(states.at[slot], states.at[slot], sa_send.at[i], sa_recv.at[i], s, h)

    def pass_state(e, i):
        slot = ring(g + n_hid, -i, n_hid) * q + j
        peer = g * q + ring(j, e, q)
        n = (e - 1) * n_hid + i
        return copy(states.at[slot], states.at[slot], sb_send.at[n], sb_recv.at[n], peer, h)

    def take_state(e, i):
        slot = ring(g + n_hid, -i, n_hid) * q + ring(j + q, -e, q)
        n = (e - 1) * n_hid + i
        return copy(states.at[slot], states.at[slot], sb_send.at[n], sb_recv.at[n], s, h)

    loop(1, n_hid, lambda i: send_state(i).start())

    def relay(i):
        @pl.when(i > 0)
        def _():
            recv_state(i).wait_recv()

        for e in range(1, q):
            pass_state(e, i).start()

    loop(0, n_hid, relay)

    def send_weight(e):
        peer = g * q + ring(j, e, q)
        return (
            copy(w1_ref, w1g.at[j], w_send.at[0, e], w_recv.at[0, e], peer, h),
            copy(w2_ref, w2g.at[j], w_send.at[1, e], w_recv.at[1, e], peer, h),
        )

    def take_weight(e):
        slot = ring(j + q, -e, q)
        return (
            copy(w1_ref, w1g.at[slot], w_send.at[0, e], w_recv.at[0, e], s, h),
            copy(w2_ref, w2g.at[slot], w_send.at[1, e], w_recv.at[1, e], s, h),
        )

    keep1 = pltpu.make_async_copy(w1_ref, w1g.at[j], w_local.at[0])
    keep2 = pltpu.make_async_copy(w2_ref, w2g.at[j], w_local.at[1])
    keep1.start()
    keep2.start()
    for e in range(1, q):
        for c in send_weight(e):
            c.start()

    for e in range(1, q):
        loop(0, n_hid, lambda i: take_state(e, i).wait_recv())

    def earlier(i, weight):
        b = n_seq - 1 - i
        valid = b < s
        tail = states[b, head : head + TAIL, :].astype(F32)
        step = tail[0:1] + tail[1:2]
        now = jnp.where(valid, weight, 0.0)
        for p in range(pairs):
            cols = slice(p * LANES, (p + 1) * LANES)
            packed = states[b, 0:head, cols].astype(F32)
            full = jnp.concatenate(
                [jnp.where(low_state, packed, 0.0), jnp.where(low_state, 0.0, packed)], axis=0
            ).astype(BF16)
            wkv[:, cols] += dot((rdec[:, cols] * now[:, cols]).astype(BF16), full)
        return jnp.where(valid, weight * step, weight)

    lax.fori_loop(0, n_seq, earlier, jnp.ones((1, width), F32))

    def finish(p, carry):
        first, second = carry
        cols = at_pair(p)
        x = wkv[:, cols]
        c = x - dot(x, same_head, precision=EXACT) * (1.0 / head)
        spread = dot(c * c, same_head, precision=EXACT) * (1.0 / head)
        n = c * lax.rsqrt(spread + EPS_GROUP) * gscale_ref[:, cols] + goffset_ref[:, cols]
        gate = gate_ref[:, cols].astype(F32)
        m = skip_ref[:, cols].astype(F32) + n * (gate / (1.0 + jnp.exp(-gate)))
        middle[:, cols] = m
        return (
            first + jnp.sum(m, axis=1, keepdims=True),
            second + jnp.sum(m * m, axis=1, keepdims=True),
        )

    zero = jnp.zeros((rows, 1), F32)
    first, second = lax.fori_loop(0, pairs, finish, (zero, zero))

    lane = iota((rows, LANES), 1)
    table = jnp.where(lane == 0, first, jnp.where(lane == 1, second, 0.0))
    stats[h] = table.T[0:8]

    def send_stat(i):
        z = ring(h, i, n_hid)
        return copy(stats.at[h], stats.at[h], st_send.at[i], st_recv.at[i], s, z)

    def take_stat(i):
        z = ring(h + n_hid, -i, n_hid)
        return copy(stats.at[z], stats.at[z], st_send.at[i], st_recv.at[i], s, h)

    loop(1, n_hid, lambda i: send_stat(i).start())
    loop(1, n_hid, lambda i: take_stat(i).wait_recv())
    sums = lax.fori_loop(0, n_hid, lambda z, a: a + stats[z], jnp.zeros((8, rows), F32))
    sums = jnp.concatenate([sums, jnp.zeros((LANES - 8, rows), F32)], axis=0).T
    full_width = width * n_hid
    mean = sums[:, 0:1] / full_width
    var = sums[:, 1:2] / full_width - mean * mean
    xn = (
        (middle[...] - mean) * lax.rsqrt(var + EPS_LAYER) * nscale_ref[...] + noffset_ref[...]
    ).astype(BF16)
    edge_out[...] = xn[rows - TAIL : rows]
    to_next = copy(edge_out, edge_in, edge_send, edge_recv, ring(s, 1, n_seq), h)

    @pl.when(s < n_seq - 1)
    def _():
        to_next.start()

    @pl.when(s == 0)
    def _():
        edge_in[...] = jnp.zeros_like(edge_in)

    @pl.when(s > 0)
    def _():
        to_next.wait_recv()

    wide = xn.astype(F32)
    carried = edge_in[...].astype(F32)[TAIL - 1 : TAIL]
    prev = jnp.where(iota((rows, width), 0) == 0, carried, pltpu.roll(wide, 1, 0))
    xk[...] = (wide + (prev - wide) * blend_ref[...]).astype(BF16)

    def send_a(i):
        return copy(
            xk, xa.at[g], a_send.at[i], a_recv.at[g], h * q + j, ring(h, i, n_hid)
        )

    def take_a(far):
        return copy(xk, xa.at[far], a_send.at[0], a_recv.at[far], s, h)

    def foreign(i):
        return jnp.logical_or(i != 0, g != h)

    def start_a(i):
        @pl.when(foreign(i))
        def _():
            send_a(i).start()

    @pl.when(g == h)
    def _():
        xa[g] = xk[...]

    loop(0, n_hid, start_a)

    keep1.wait()
    keep2.wait()
    for e in range(1, q):
        for c in take_weight(e):
            c.wait_recv()

    tile = 256 if units % 256 == 0 else units

    def partial_b(far):
        def column(c):
            cols = pl.ds(pl.multiple_of(c * tile, tile), tile) if tile < units else slice(None)
            total_tile = dot(xa[far, :, 0:depth], w1g[0, :, cols])
            for e in range(1, q):
                total_tile += dot(xa[far, :, e * depth : (e + 1) * depth], w1g[e, :, cols])
            part_out[far, :, cols] = total_tile.astype(BF16)

        loop(0, units // tile, column)

    def send_b(far):
        return copy(
            part_out.at[far], part_in.at[g], b_send.at[far], b_recv.at[g], far * q + j, h
        )

    def take_b(far):
        return copy(part_out.at[far], part_in.at[far], b_send.at[far], b_recv.at[far], s, h)

    def phase_b(i):
        far = ring(g, i + 1, n_hid)

        @pl.when(jnp.logical_or(far != g, g != h))
        def _():
            take_a(far).wait_recv()

        partial_b(far)

        @pl.when(far != g)
        def _():
            send_b(far).start()

    loop(0, n_hid, phase_b)
    loop(1, n_hid, lambda i: take_b(ring(g, i, n_hid)).wait_recv())

    def activate(c):
        cols = pl.ds(pl.multiple_of(c * tile, tile), tile) if tile < units else slice(None)
        pre = lax.fori_loop(
            1,
            n_hid,
            lambda i, a: a + part_in[ring(g, i, n_hid), :, cols].astype(F32),
            part_out[g, :, cols].astype(F32),
        )
        hidden[g, :, cols] = jnp.square(jnp.maximum(pre, 0.0)).astype(BF16)

    loop(0, units // tile, activate)

    def send_c(far):
        return copy(hidden.at[g], hidden.at[g], c_send.at[far], c_recv.at[g], far * q + j, h)

    def take_c(far):
        return copy(hidden.at[far], hidden.at[far], c_send.at[far], c_recv.at[far], s, h)

    loop(1, n_hid, lambda i: send_c(ring(g, i, n_hid)).start())

    depth_tile = 256 if depth % 256 == 0 else depth

    def partial_d(far):
        for e in range(q):
            for c in range(depth // depth_tile):
                lo = c * depth_tile
                col = e * depth + lo
                down_out[far, :, col : col + depth_tile] = dot(
                    hidden[far], w2g[e, lo : lo + depth_tile, :], ((1,), (1,))
                ).astype(BF16)

    def send_d(far):
        return copy(
            down_out.at[far], down_in.at[h], d_send.at[far], d_recv.at[h], far * q + j, g
        )

    def take_d(z):
        return copy(down_out.at[z], down_in.at[z], d_send.at[z], d_recv.at[z], s, h)

    def phase_d(i):
        far = ring(g, i, n_hid)

        @pl.when(i > 0)
        def _():
            take_c(far).wait_recv()

        partial_d(far)

        @pl.when(foreign(i))
        def _():
            send_d(far).start()

        @pl.when(jnp.logical_not(foreign(i)))
        def _():
            down_in[h] = down_out[far]

    loop(0, n_hid, phase_d)

    def end_d(z):
        @pl.when(jnp.logical_or(z != h, g != h))
        def _():
            take_d(z).wait_recv()

    loop(0, n_hid, end_d)

    def result(p):
        cols = at_pair(p)
        down = lax.fori_loop(
            0,
            n_hid,
            lambda z, a: a + down_in[z, :, cols].astype(F32),
            jnp.zeros((rows, LANES), F32),
        )
        out_ref[:, cols] = (middle[:, cols] + down).astype(BF16)

    loop(0, pairs, result)

    loop(1, n_hid, lambda i: send_state(i).wait_send())
    for e in range(1, q):
        loop(0, n_hid, lambda i: pass_state(e, i).wait_send())
        for c in send_weight(e):
            c.wait_send()
    loop(1, n_hid, lambda i: send_stat(i).wait_send())

    @pl.when(s < n_seq - 1)
    def _():
        to_next.wait_send()

    def end_sends(i):
        far = ring(g, i, n_hid)

        @pl.when(foreign(i))
        def _():
            send_a(i).wait_send()
            send_d(far).wait_send()

        @pl.when(i > 0)
        def _():
            send_b(far).wait_send()
            send_c(far).wait_send()

    loop(0, n_hid, end_sends)


def local(n_seq, n_hid, *args):
    skip = args[0]
    boost = args[6]
    w1 = args[12]
    rows, width = skip.shape
    heads, head = boost.shape
    depth, units = w1.shape
    q = n_seq // n_hid
    vmem = pl.BlockSpec(memory_space=pltpu.VMEM)
    anywhere = pl.BlockSpec(memory_space=pl.ANY)
    dma = pltpu.SemaphoreType.DMA
    operands = list(args[:6]) + [a.reshape(1, width) for a in args[6:12]] + list(args[12:])
    return pl.pallas_call(
        functools.partial(block_kernel, n_seq, n_hid, head),
        out_shape=jax.ShapeDtypeStruct((rows, width), BF16),
        in_specs=[vmem] * 12 + [anywhere] * 2,
        out_specs=vmem,
        scratch_shapes=[
            pltpu.VMEM((n_seq, head + TAIL, width), BF16),
            pltpu.VMEM((rows, width), F32),
            pltpu.VMEM((rows, width), F32),
            pltpu.VMEM((rows, width), F32),
            pltpu.VMEM((rows, width), BF16),
            pltpu.VMEM((rows, width), BF16),
            pltpu.VMEM((rows, width), F32),
            pltpu.VMEM((n_hid, 8, rows), F32),
            pltpu.VMEM((TAIL, width), BF16),
            pltpu.VMEM((TAIL, width), BF16),
            pltpu.VMEM((rows, width), BF16),
            pltpu.VMEM((n_hid, rows, width), BF16),
            pltpu.VMEM((q, depth, units), BF16),
            pltpu.VMEM((q, depth, units), BF16),
            pltpu.VMEM((n_hid, rows, units), BF16),
            pltpu.VMEM((n_hid, rows, units), BF16),
            pltpu.VMEM((n_hid, rows, units), BF16),
            pltpu.VMEM((n_hid, rows, width), BF16),
            pltpu.VMEM((n_hid, rows, width), BF16),
            dma((n_hid,)),
            dma((n_hid,)),
            dma((q * n_hid,)),
            dma((q * n_hid,)),
            dma((n_hid,)),
            dma((n_hid,)),
            dma,
            dma,
            dma((2, q)),
            dma((2, q)),
            dma((2,)),
            dma((n_hid,)),
            dma((n_hid,)),
            dma((n_hid,)),
            dma((n_hid,)),
            dma((n_hid,)),
            dma((n_hid,)),
            dma((n_hid,)),
            dma((n_hid,)),
        ],
        compiler_params=pltpu.CompilerParams(
            collective_id=0, has_side_effects=True, vmem_limit_bytes=48 * 2**20
        ),
    )(*operands)


def solution(mesh):
    return jax.shard_map(
        functools.partial(local, mesh.shape["seq"], mesh.shape["hid"]),
        mesh=mesh,
        in_specs=(P("seq", "hid"),) * 6
        + (P("hid", None),)
        + (P("hid"),) * 5
        + (P("seq", "hid"),) * 2,
        out_specs=P("seq", "hid"),
        check_vma=False,
    )
```

```python
import functools

import jax
import jax.numpy as jnp
from jax import lax
from jax.experimental import pallas as pl
from jax.experimental.pallas import tpu as pltpu
from jax.sharding import PartitionSpec as P

EPS_GROUP = 0.00064
EPS_LAYER = 1e-05
F32 = jnp.float32
BF16 = jnp.bfloat16
LANES = 128
TAIL = 16


def dot(a, b, dims=((1,), (0,))):
    return lax.dot_general(a, b, (dims, ((), ())), preferred_element_type=F32)


def iota(shape, axis):
    return lax.broadcasted_iota(jnp.int32, shape, axis)


def halves(x):
    high = x.astype(BF16)
    return high, x - high.astype(F32)


def head_sums(x, same_head):
    high, rest = halves(x)
    return dot(high, same_head) + dot(rest.astype(BF16), same_head)


def block_kernel(
    n_seq,
    n_hid,
    head,
    skip_hbm,
    r_hbm,
    k_hbm,
    v_hbm,
    gate_hbm,
    logit_hbm,
    boost_hbm,
    gscale_hbm,
    goffset_hbm,
    nscale_hbm,
    noffset_hbm,
    blend_hbm,
    w1_ref,
    w2_ref,
    out_ref,
    skip_ref,
    r_ref,
    k_ref,
    v_ref,
    gate_ref,
    logit_ref,
    boost_ref,
    gscale_ref,
    goffset_ref,
    nscale_ref,
    noffset_ref,
    blend_ref,
    in_sems,
    states,
    wkv,
    rdec,
    rmid,
    kmid,
    kend,
    middle,
    stats,
    edge_out,
    edge_in,
    reach,
    xk,
    planes,
    xa,
    w1g,
    w2g,
    part_out,
    part_in,
    hidden,
    down_out,
    down_mid,
    down_in,
    sa_send,
    sa_recv,
    sb_send,
    sb_recv,
    st_send,
    st_recv,
    edge_send,
    edge_recv,
    w_send,
    w_recv,
    w_local,
    z_send,
    z_recv,
    a_send,
    a_recv,
    b_send,
    b_recv,
    c_send,
    c_recv,
    d_send,
    d_recv,
    y_send,
    y_recv,
):
    rows, width = skip_ref.shape
    depth, units = w1_ref.shape
    q = n_seq // n_hid
    pairs = width // LANES
    s = lax.axis_index("seq")
    h = lax.axis_index("hid")
    g = lax.div(s, q)
    j = lax.rem(s, q)

    def at(seq, hid):
        return {"seq": seq, "hid": hid}

    def copy(src, dst, send, recv, seq, hid):
        return pltpu.make_async_remote_copy(
            src_ref=src,
            dst_ref=dst,
            send_sem=send,
            recv_sem=recv,
            device_id=at(seq, hid),
            device_id_type=pl.DeviceIdType.MESH,
        )

    def ring(base, i, size):
        return lax.rem(base + i, size)

    def loop(start, stop, body):
        def step(i, carry):
            body(i)
            return carry

        lax.fori_loop(start, stop, step, 0)

    arrivals = [
        pltpu.make_async_copy(source, target, in_sems.at[n])
        for n, (source, target) in enumerate(
            (
                (skip_hbm, skip_ref),
                (r_hbm, r_ref),
                (k_hbm, k_ref),
                (v_hbm, v_ref),
                (gate_hbm, gate_ref),
                (logit_hbm, logit_ref),
                (boost_hbm, boost_ref),
                (gscale_hbm, gscale_ref),
                (goffset_hbm, goffset_ref),
                (nscale_hbm, nscale_ref),
                (noffset_hbm, noffset_ref),
                (blend_hbm, blend_ref),
            )
        )
    ]
    for c in arrivals:
        c.start()
    keep1 = pltpu.make_async_copy(w1_ref, w1g.at[j], w_local.at[0])
    keep2 = pltpu.make_async_copy(w2_ref, w2g.at[j], w_local.at[1])
    keep1.start()
    keep2.start()

    barrier = pltpu.get_barrier_semaphore()

    def greet(seq, hid):
        pl.semaphore_signal(
            barrier, inc=1, device_id=at(seq, hid), device_id_type=pl.DeviceIdType.MESH
        )

    loop(1, n_seq, lambda i: greet(ring(s, i, n_seq), h))
    loop(1, n_hid, lambda i: greet(s, ring(h, i, n_hid)))

    for c in arrivals:
        c.wait()

    logw = -jnp.exp(logit_ref[...])
    tri = (iota((rows, rows), 0) >= iota((rows, rows), 1)).astype(F32).astype(BF16)
    top, rest = halves(logw)
    mid, rest = halves(rest)
    inclusive = dot(tri, top) + (dot(tri, mid) + dot(tri, rest.astype(BF16)))
    exclusive = inclusive - logw
    centre_row = inclusive[rows // 2 - 1 : rows // 2]
    total = inclusive[rows - 1 : rows]
    r_all = r_ref[...].astype(F32)
    k_all = k_ref[...].astype(F32)
    rdec[...] = r_all * jnp.exp(exclusive)
    rmid[...] = r_all * jnp.exp(exclusive - centre_row)
    kmid[...] = (k_all * jnp.exp(centre_row - inclusive)).astype(BF16)
    kend[...] = (k_all * jnp.exp(total - inclusive)).astype(BF16)
    decay = jnp.exp(total)
    decay_high = decay.astype(BF16).astype(F32)
    tail_row = iota((TAIL, width), 0)
    states[s, head : head + TAIL, :] = jnp.where(
        tail_row == 0, decay_high, jnp.where(tail_row == 1, decay - decay_high, 0.0)
    ).astype(BF16)

    low = iota((rows, LANES), 1) < head
    low_state = iota((head, LANES), 1) < head
    strict = iota((rows, rows), 0) > iota((rows, rows), 1)
    same = (iota((LANES, LANES), 0) < head) == (iota((LANES, LANES), 1) < head)
    same_head = same.astype(F32).astype(BF16)

    def at_pair(p):
        return pl.ds(pl.multiple_of(p * LANES, LANES), LANES)

    def chunk(p):
        cols = at_pair(p)
        rm = rmid[:, cols]
        km = kmid[:, cols]
        vv = v_ref[:, cols]
        vf = vv.astype(F32)
        first = dot(jnp.where(low, rm, 0.0).astype(BF16), km, ((1,), (1,)))
        second = dot(jnp.where(low, 0.0, rm).astype(BF16), km, ((1,), (1,)))
        first = jnp.where(strict, first, 0.0).astype(BF16)
        second = jnp.where(strict, second, 0.0).astype(BF16)
        own = r_ref[:, cols].astype(F32) * boost_ref[:, cols] * k_ref[:, cols].astype(F32)
        wkv[:, cols] = (
            dot(first, jnp.where(low, vf, 0.0).astype(BF16))
            + dot(second, jnp.where(low, 0.0, vf).astype(BF16))
            + head_sums(own, same_head) * vf
        )
        outer = dot(kend[:, cols], vv, ((0,), (0,)))
        states[s, 0:head, cols] = jnp.where(
            low_state, outer[0:head], outer[head : 2 * head]
        ).astype(BF16)

    several = max(n for n in (1, 2, 4) if pairs % n == 0)

    def chunks(i):
        for n in range(several):
            chunk(i * several + n)

    loop(0, pairs // several, chunks)

    pl.semaphore_wait(barrier, (n_seq - 1) + (n_hid - 1))

    def send_state(i):
        peer = ring(g, i, n_hid) * q + j
        return copy(states.at[s], states.at[s], sa_send.at[i], sa_recv.at[i], peer, h)

    def recv_state(i):
        slot = ring(g + n_hid, -i, n_hid) * q + j
        return copy(states.at[slot], states.at[slot], sa_send.at[i], sa_recv.at[i], s, h)

    def pass_state(e, i):
        slot = ring(g + n_hid, -i, n_hid) * q + j
        peer = g * q + ring(j, e, q)
        n = (e - 1) * n_hid + i
        return copy(states.at[slot], states.at[slot], sb_send.at[n], sb_recv.at[n], peer, h)

    def take_state(e, i):
        slot = ring(g + n_hid, -i, n_hid) * q + ring(j + q, -e, q)
        n = (e - 1) * n_hid + i
        return copy(states.at[slot], states.at[slot], sb_send.at[n], sb_recv.at[n], s, h)

    loop(1, n_hid, lambda i: send_state(i).start())

    def relay(i):
        @pl.when(i > 0)
        def _():
            recv_state(i).wait_recv()

        for e in range(1, q):
            pass_state(e, i).start()

    loop(0, n_hid, relay)

    def send_weight(e):
        peer = g * q + ring(j, e, q)
        return (
            copy(w1_ref, w1g.at[j], w_send.at[0, e], w_recv.at[0, e], peer, h),
            copy(w2_ref, w2g.at[j], w_send.at[1, e], w_recv.at[1, e], peer, h),
        )

    def take_weight(e):
        slot = ring(j + q, -e, q)
        return (
            copy(w1_ref, w1g.at[slot], w_send.at[0, e], w_recv.at[0, e], s, h),
            copy(w2_ref, w2g.at[slot], w_send.at[1, e], w_recv.at[1, e], s, h),
        )

    for e in range(1, q):
        for c in send_weight(e):
            c.start()

    for e in range(1, q):
        loop(0, n_hid, lambda i: take_state(e, i).wait_recv())

    weight = jnp.ones((1, width), F32)
    for b in reversed(range(n_seq)):
        valid = b < s
        tail = states[b, head : head + TAIL, :].astype(F32)
        reach[b : b + 1, :] = jnp.where(valid, weight, 0.0)
        weight = jnp.where(valid, weight * (tail[0:1] + tail[1:2]), weight)

    def earlier(p):
        cols = at_pair(p)
        rd = rdec[:, cols]
        total = wkv[:, cols]
        for start in range(0, n_seq, n_hid):
            left = []
            right = []
            for b in range(start, start + n_hid):
                packed = states[b, 0:head, cols].astype(F32)
                right.append(jnp.where(low_state, packed, 0.0).astype(BF16))
                right.append(jnp.where(low_state, 0.0, packed).astype(BF16))
                left.append((rd * reach[b : b + 1, cols]).astype(BF16))
            total += dot(jnp.concatenate(left, axis=1), jnp.concatenate(right, axis=0))
        wkv[:, cols] = total

    def earliers(i):
        for n in range(several):
            earlier(i * several + n)

    loop(0, pairs // several, earliers)

    def finish(p, carry):
        first, second = carry
        cols = at_pair(p)
        x = wkv[:, cols]
        c = x - head_sums(x, same_head) * (1.0 / head)
        spread = head_sums(c * c, same_head) * (1.0 / head)
        n = c * lax.rsqrt(spread + EPS_GROUP) * gscale_ref[:, cols] + goffset_ref[:, cols]
        gate = gate_ref[:, cols].astype(F32)
        m = skip_ref[:, cols].astype(F32) + n * (gate / (1.0 + jnp.exp(-gate)))
        middle[:, cols] = m
        return (
            first + jnp.sum(m, axis=1, keepdims=True),
            second + jnp.sum(m * m, axis=1, keepdims=True),
        )

    zero = jnp.zeros((rows, 1), F32)

    def finishes(i, carry):
        for n in range(several):
            carry = finish(i * several + n, carry)
        return carry

    first, second = lax.fori_loop(0, pairs // several, finishes, (zero, zero))

    lane = iota((rows, LANES), 1)
    table = jnp.where(lane == 0, first, jnp.where(lane == 1, second, 0.0))
    stats[h] = table.T[0:8]

    def send_stat(i):
        z = ring(h, i, n_hid)
        return copy(stats.at[h], stats.at[h], st_send.at[i], st_recv.at[i], s, z)

    def take_stat(i):
        z = ring(h + n_hid, -i, n_hid)
        return copy(stats.at[z], stats.at[z], st_send.at[i], st_recv.at[i], s, h)

    loop(1, n_hid, lambda i: send_stat(i).start())
    loop(1, n_hid, lambda i: take_stat(i).wait_recv())
    sums = lax.fori_loop(0, n_hid, lambda z, a: a + stats[z], jnp.zeros((8, rows), F32))
    sums = jnp.concatenate([sums, jnp.zeros((LANES - 8, rows), F32)], axis=0).T
    full_width = width * n_hid
    mean = sums[:, 0:1] / full_width
    var = sums[:, 1:2] / full_width - mean * mean
    xn = (
        (middle[...] - mean) * lax.rsqrt(var + EPS_LAYER) * nscale_ref[...] + noffset_ref[...]
    ).astype(BF16)
    edge_out[...] = xn[rows - TAIL : rows]
    to_next = copy(edge_out, edge_in, edge_send, edge_recv, ring(s, 1, n_seq), h)

    @pl.when(s < n_seq - 1)
    def _():
        to_next.start()

    @pl.when(s == 0)
    def _():
        edge_in[...] = jnp.zeros_like(edge_in)

    @pl.when(s > 0)
    def _():
        to_next.wait_recv()

    wide = xn.astype(F32)
    carried = edge_in[...].astype(F32)[TAIL - 1 : TAIL]
    prev = jnp.where(iota((rows, width), 0) == 0, carried, pltpu.roll(wide, 1, 0))
    xk[...] = (wide + (prev - wide) * blend_ref[...]).astype(BF16)

    def send_z(i):
        z = ring(h, i, n_hid)
        return copy(xk, planes.at[h], z_send.at[i], z_recv.at[i], s, z)

    def take_z(i):
        z = ring(h + n_hid, -i, n_hid)
        return copy(xk, planes.at[z], z_send.at[i], z_recv.at[i], s, h)

    def send_a(far):
        return copy(planes.at[far], xa.at[g], a_send.at[far], a_recv.at[g], far * q + j, h)

    def take_a(far):
        return copy(planes.at[far], xa.at[far], a_send.at[far], a_recv.at[far], s, h)

    loop(1, n_hid, lambda i: send_z(i).start())
    planes[h] = xk[...]

    def start_a(i):
        z = ring(h + n_hid, -i, n_hid)

        @pl.when(i > 0)
        def _():
            take_z(i).wait_recv()

        @pl.when(z != g)
        def _():
            send_a(z).start()

        @pl.when(z == g)
        def _():
            xa[g] = planes[z]

    loop(0, n_hid, start_a)

    keep1.wait()
    keep2.wait()
    for e in range(1, q):
        for c in take_weight(e):
            c.wait_recv()

    tile = 256 if units % 256 == 0 else units

    def partial_b(far):
        def column(c):
            cols = pl.ds(pl.multiple_of(c * tile, tile), tile) if tile < units else slice(None)
            total_tile = dot(xa[far, :, 0:depth], w1g[0, :, cols])
            for e in range(1, q):
                total_tile += dot(xa[far, :, e * depth : (e + 1) * depth], w1g[e, :, cols])
            part_out[far, :, cols] = total_tile.astype(BF16)

        loop(0, units // tile, column)

    def send_b(far):
        return copy(
            part_out.at[far], part_in.at[g], b_send.at[far], b_recv.at[g], far * q + j, h
        )

    def take_b(far):
        return copy(part_out.at[far], part_in.at[far], b_send.at[far], b_recv.at[far], s, h)

    def phase_b(i):
        far = ring(g, i + 1, n_hid)

        @pl.when(far != g)
        def _():
            take_a(far).wait_recv()

        partial_b(far)

        @pl.when(far != g)
        def _():
            send_b(far).start()

    loop(0, n_hid, phase_b)
    loop(1, n_hid, lambda i: take_b(ring(g, i, n_hid)).wait_recv())

    def activate(c):
        cols = pl.ds(pl.multiple_of(c * tile, tile), tile) if tile < units else slice(None)
        pre = lax.fori_loop(
            1,
            n_hid,
            lambda i, a: a + part_in[ring(g, i, n_hid), :, cols].astype(F32),
            part_out[g, :, cols].astype(F32),
        )
        hidden[g, :, cols] = jnp.square(jnp.maximum(pre, 0.0)).astype(BF16)

    loop(0, units // tile, activate)

    def send_c(far):
        return copy(hidden.at[g], hidden.at[g], c_send.at[far], c_recv.at[g], far * q + j, h)

    def take_c(far):
        return copy(hidden.at[far], hidden.at[far], c_send.at[far], c_recv.at[far], s, h)

    loop(1, n_hid, lambda i: send_c(ring(g, i, n_hid)).start())

    depth_tile = 256 if depth % 256 == 0 else depth

    def partial_d(far):
        for e in range(q):
            for c in range(depth // depth_tile):
                lo = c * depth_tile
                col = e * depth + lo
                down_out[far, :, col : col + depth_tile] = dot(
                    hidden[far], w2g[e, lo : lo + depth_tile, :], ((1,), (1,))
                ).astype(BF16)

    def send_d(far):
        return copy(
            down_out.at[far], down_mid.at[g], d_send.at[far], d_recv.at[g], far * q + j, h
        )

    def take_d(far):
        return copy(
            down_out.at[far], down_mid.at[far], d_send.at[far], d_recv.at[far], s, h
        )

    def send_y(far):
        return copy(down_mid.at[far], down_in.at[h], y_send.at[far], y_recv.at[h], s, far)

    def take_y(z):
        return copy(down_mid.at[z], down_in.at[z], y_send.at[z], y_recv.at[z], s, h)

    def onward(far):
        @pl.when(far != h)
        def _():
            send_y(far).start()

        @pl.when(far == h)
        def _():
            down_in[h] = down_mid[far]

    partial_d(g)
    down_mid[g] = down_out[g]
    onward(g)

    def phase_d(i):
        far = ring(g, i, n_hid)
        take_c(far).wait_recv()
        partial_d(far)
        send_d(far).start()

    loop(1, n_hid, phase_d)

    def phase_y(i):
        far = ring(g, i, n_hid)
        take_d(far).wait_recv()
        onward(far)

    loop(1, n_hid, phase_y)
    loop(1, n_hid, lambda i: take_y(ring(h, i, n_hid)).wait_recv())

    def result(p):
        cols = at_pair(p)
        down = lax.fori_loop(
            0,
            n_hid,
            lambda z, a: a + down_in[z, :, cols].astype(F32),
            jnp.zeros((rows, LANES), F32),
        )
        out_ref[:, cols] = (middle[:, cols] + down).astype(BF16)

    loop(0, pairs, result)

    loop(1, n_hid, lambda i: send_state(i).wait_send())
    for e in range(1, q):
        loop(0, n_hid, lambda i: pass_state(e, i).wait_send())
        for c in send_weight(e):
            c.wait_send()
    loop(1, n_hid, lambda i: send_stat(i).wait_send())

    @pl.when(s < n_seq - 1)
    def _():
        to_next.wait_send()

    def end_sends(i):
        far = ring(g, i, n_hid)

        @pl.when(i > 0)
        def _():
            send_z(i).wait_send()
            send_a(far).wait_send()
            send_b(far).wait_send()
            send_c(far).wait_send()
            send_d(far).wait_send()
            send_y(ring(h, i, n_hid)).wait_send()

    loop(0, n_hid, end_sends)


def local(n_seq, n_hid, *args):
    skip = args[0]
    boost = args[6]
    w1 = args[12]
    rows, width = skip.shape
    heads, head = boost.shape
    depth, units = w1.shape
    q = n_seq // n_hid
    vmem = pl.BlockSpec(memory_space=pltpu.VMEM)
    anywhere = pl.BlockSpec(memory_space=pl.ANY)
    dma = pltpu.SemaphoreType.DMA
    operands = list(args[:6]) + [a.reshape(1, width) for a in args[6:12]] + list(args[12:])
    return pl.pallas_call(
        functools.partial(block_kernel, n_seq, n_hid, head),
        out_shape=jax.ShapeDtypeStruct((rows, width), BF16),
        in_specs=[anywhere] * 14,
        out_specs=vmem,
        scratch_shapes=[pltpu.VMEM(a.shape, a.dtype) for a in operands[:12]]
        + [
            dma((12,)),
            pltpu.VMEM((n_seq, head + TAIL, width), BF16),
            pltpu.VMEM((rows, width), F32),
            pltpu.VMEM((rows, width), F32),
            pltpu.VMEM((rows, width), F32),
            pltpu.VMEM((rows, width), BF16),
            pltpu.VMEM((rows, width), BF16),
            pltpu.VMEM((rows, width), F32),
            pltpu.VMEM((n_hid, 8, rows), F32),
            pltpu.VMEM((TAIL, width), BF16),
            pltpu.VMEM((TAIL, width), BF16),
            pltpu.VMEM((n_seq, width), F32),
            pltpu.VMEM((rows, width), BF16),
            pltpu.VMEM((n_hid, rows, width), BF16),
            pltpu.VMEM((n_hid, rows, width), BF16),
            pltpu.VMEM((q, depth, units), BF16),
            pltpu.VMEM((q, depth, units), BF16),
            pltpu.VMEM((n_hid, rows, units), BF16),
            pltpu.VMEM((n_hid, rows, units), BF16),
            pltpu.VMEM((n_hid, rows, units), BF16),
            pltpu.VMEM((n_hid, rows, width), BF16),
            pltpu.VMEM((n_hid, rows, width), BF16),
            pltpu.VMEM((n_hid, rows, width), BF16),
            dma((n_hid,)),
            dma((n_hid,)),
            dma((q * n_hid,)),
            dma((q * n_hid,)),
            dma((n_hid,)),
            dma((n_hid,)),
            dma,
            dma,
            dma((2, q)),
            dma((2, q)),
            dma((2,)),
            dma((n_hid,)),
            dma((n_hid,)),
            dma((n_hid,)),
            dma((n_hid,)),
            dma((n_hid,)),
            dma((n_hid,)),
            dma((n_hid,)),
            dma((n_hid,)),
            dma((n_hid,)),
            dma((n_hid,)),
            dma((n_hid,)),
            dma((n_hid,)),
        ],
        compiler_params=pltpu.CompilerParams(
            collective_id=0, has_side_effects=True, vmem_limit_bytes=60 * 2**20
        ),
    )(*operands)


def solution(mesh):
    return jax.shard_map(
        functools.partial(local, mesh.shape["seq"], mesh.shape["hid"]),
        mesh=mesh,
        in_specs=(P("seq", "hid"),) * 6
        + (P("hid", None),)
        + (P("hid"),) * 5
        + (P("seq", "hid"),) * 2,
        out_specs=P("seq", "hid"),
        check_vma=False,
    )
```

```python
import functools

import jax
import jax.numpy as jnp
from jax import lax
from jax.experimental import pallas as pl
from jax.experimental.pallas import tpu as pltpu
from jax.sharding import PartitionSpec as P

EPS_GROUP = 0.00064
EPS_LAYER = 1e-05
F32 = jnp.float32
BF16 = jnp.bfloat16
LANES = 128
TAIL = 16


def dot(a, b, dims=((1,), (0,))):
    return lax.dot_general(a, b, (dims, ((), ())), preferred_element_type=F32)


def iota(shape, axis):
    return lax.broadcasted_iota(jnp.int32, shape, axis)


def halves(x):
    high = x.astype(BF16)
    return high, x - high.astype(F32)


def head_sums(x, same_head):
    high, rest = halves(x)
    return dot(high, same_head) + dot(rest.astype(BF16), same_head)


def block_kernel(
    n_seq,
    n_hid,
    head,
    skip_hbm,
    r_hbm,
    k_hbm,
    v_hbm,
    gate_hbm,
    logit_hbm,
    boost_hbm,
    gscale_hbm,
    goffset_hbm,
    nscale_hbm,
    noffset_hbm,
    blend_hbm,
    w1_ref,
    w2_ref,
    out_ref,
    skip_ref,
    r_ref,
    k_ref,
    v_ref,
    gate_ref,
    logit_ref,
    boost_ref,
    gscale_ref,
    goffset_ref,
    nscale_ref,
    noffset_ref,
    blend_ref,
    in_sems,
    states,
    wkv,
    rdec,
    rmid,
    kmid,
    kend,
    middle,
    stats,
    edge_out,
    edge_in,
    reach,
    xk,
    planes,
    xa,
    w1g,
    w2g,
    part_out,
    part_in,
    hidden,
    down_out,
    down_mid,
    down_in,
    sa_send,
    sa_recv,
    sb_send,
    sb_recv,
    st_send,
    st_recv,
    edge_send,
    edge_recv,
    w_send,
    w_recv,
    w_local,
    z_send,
    z_recv,
    a_send,
    a_recv,
    b_send,
    b_recv,
    c_send,
    c_recv,
    d_send,
    d_recv,
    y_send,
    y_recv,
):
    rows, width = skip_ref.shape
    depth, units = w1_ref.shape
    q = n_seq // n_hid
    pairs = width // LANES
    half = rows // 2
    s = lax.axis_index("seq")
    h = lax.axis_index("hid")
    g = lax.div(s, q)
    j = lax.rem(s, q)

    def at(seq, hid):
        return {"seq": seq, "hid": hid}

    def copy(src, dst, send, recv, seq, hid):
        return pltpu.make_async_remote_copy(
            src_ref=src,
            dst_ref=dst,
            send_sem=send,
            recv_sem=recv,
            device_id=at(seq, hid),
            device_id_type=pl.DeviceIdType.MESH,
        )

    def ring(base, i, size):
        return lax.rem(base + i, size)

    def loop(start, stop, body):
        def step(i, carry):
            body(i)
            return carry

        lax.fori_loop(start, stop, step, 0)

    arrivals = [
        pltpu.make_async_copy(source, target, in_sems.at[n])
        for n, (source, target) in enumerate(
            (
                (skip_hbm, skip_ref),
                (r_hbm, r_ref),
                (k_hbm, k_ref),
                (v_hbm, v_ref),
                (gate_hbm, gate_ref),
                (logit_hbm, logit_ref),
                (boost_hbm, boost_ref),
                (gscale_hbm, gscale_ref),
                (goffset_hbm, goffset_ref),
                (nscale_hbm, nscale_ref),
                (noffset_hbm, noffset_ref),
                (blend_hbm, blend_ref),
            )
        )
    ]
    for c in arrivals:
        c.start()
    keep1 = pltpu.make_async_copy(w1_ref, w1g.at[j], w_local.at[0])
    keep2 = pltpu.make_async_copy(w2_ref, w2g.at[j], w_local.at[1])
    keep1.start()
    keep2.start()

    barrier = pltpu.get_barrier_semaphore()

    def greet(seq, hid):
        pl.semaphore_signal(
            barrier, inc=1, device_id=at(seq, hid), device_id_type=pl.DeviceIdType.MESH
        )

    loop(1, n_seq, lambda i: greet(ring(s, i, n_seq), h))
    loop(1, n_hid, lambda i: greet(s, ring(h, i, n_hid)))

    for c in arrivals:
        c.wait()

    logw = -jnp.exp(logit_ref[...])
    tri = (iota((rows, rows), 0) >= iota((rows, rows), 1)).astype(F32).astype(BF16)
    top, rest = halves(logw)
    mid, rest = halves(rest)
    inclusive = dot(tri, top) + (dot(tri, mid) + dot(tri, rest.astype(BF16)))
    exclusive = inclusive - logw
    centre_row = inclusive[rows // 2 - 1 : rows // 2]
    total = inclusive[rows - 1 : rows]
    r_all = r_ref[...].astype(F32)
    k_all = k_ref[...].astype(F32)
    rdec[...] = r_all * jnp.exp(exclusive)
    rmid[...] = r_all * jnp.exp(exclusive - centre_row)
    kmid[...] = (k_all * jnp.exp(centre_row - inclusive)).astype(BF16)
    kend[...] = (k_all * jnp.exp(total - inclusive)).astype(BF16)
    decay = jnp.exp(total)
    decay_high = decay.astype(BF16).astype(F32)
    tail_row = iota((TAIL, width), 0)
    states[s, head : head + TAIL, :] = jnp.where(
        tail_row == 0, decay_high, jnp.where(tail_row == 1, decay - decay_high, 0.0)
    ).astype(BF16)

    low = iota((rows, LANES), 1) < head
    low_state = iota((head, LANES), 1) < head
    strict = iota((rows, rows), 0) > iota((rows, rows), 1)
    same = (iota((LANES, LANES), 0) < head) == (iota((LANES, LANES), 1) < head)
    same_head = same.astype(F32).astype(BF16)

    def at_pair(p):
        return pl.ds(pl.multiple_of(p * LANES, LANES), LANES)

    def chunk(p):
        cols = at_pair(p)
        rm = rmid[:, cols]
        km = kmid[:, cols]
        vv = v_ref[:, cols]
        vf = vv.astype(F32)
        first = dot(jnp.where(low, rm, 0.0).astype(BF16), km, ((1,), (1,)))
        second = dot(jnp.where(low, 0.0, rm).astype(BF16), km, ((1,), (1,)))
        first = jnp.where(strict, first, 0.0).astype(BF16)
        second = jnp.where(strict, second, 0.0).astype(BF16)
        own = r_ref[:, cols].astype(F32) * boost_ref[:, cols] * k_ref[:, cols].astype(F32)
        wkv[:, cols] = (
            dot(first, jnp.where(low, vf, 0.0).astype(BF16))
            + dot(second, jnp.where(low, 0.0, vf).astype(BF16))
            + head_sums(own, same_head) * vf
        )
        outer = dot(kend[:, cols], vv, ((0,), (0,)))
        states[s, 0:head, cols] = jnp.where(
            low_state, outer[0:head], outer[head : 2 * head]
        ).astype(BF16)

    several = max(n for n in (1, 2, 4) if pairs % n == 0)

    def chunks(i):
        for n in range(several):
            chunk(i * several + n)

    loop(0, pairs // several, chunks)

    pl.semaphore_wait(barrier, (n_seq - 1) + (n_hid - 1))

    def send_state(i):
        peer = ring(g, i, n_hid) * q + j
        return copy(states.at[s], states.at[s], sa_send.at[i], sa_recv.at[i], peer, h)

    def recv_state(i):
        slot = ring(g + n_hid, -i, n_hid) * q + j
        return copy(states.at[slot], states.at[slot], sa_send.at[i], sa_recv.at[i], s, h)

    def pass_state(e, i):
        slot = ring(g + n_hid, -i, n_hid) * q + j
        peer = g * q + ring(j, e, q)
        n = (e - 1) * n_hid + i
        return copy(states.at[slot], states.at[slot], sb_send.at[n], sb_recv.at[n], peer, h)

    def take_state(e, i):
        slot = ring(g + n_hid, -i, n_hid) * q + ring(j + q, -e, q)
        n = (e - 1) * n_hid + i
        return copy(states.at[slot], states.at[slot], sb_send.at[n], sb_recv.at[n], s, h)

    loop(1, n_hid, lambda i: send_state(i).start())

    def relay(i):
        @pl.when(i > 0)
        def _():
            recv_state(i).wait_recv()

        for e in range(1, q):
            pass_state(e, i).start()

    loop(0, n_hid, relay)

    def send_weight(e):
        peer = g * q + ring(j, e, q)
        return (
            copy(w1_ref, w1g.at[j], w_send.at[0, e], w_recv.at[0, e], peer, h),
            copy(w2_ref, w2g.at[j], w_send.at[1, e], w_recv.at[1, e], peer, h),
        )

    def take_weight(e):
        slot = ring(j + q, -e, q)
        return (
            copy(w1_ref, w1g.at[slot], w_send.at[0, e], w_recv.at[0, e], s, h),
            copy(w2_ref, w2g.at[slot], w_send.at[1, e], w_recv.at[1, e], s, h),
        )

    for e in range(1, q):
        for c in send_weight(e):
            c.start()

    for e in range(1, q):
        loop(0, n_hid, lambda i: take_state(e, i).wait_recv())

    weight = jnp.ones((1, width), F32)
    for b in reversed(range(n_seq)):
        valid = b < s
        tail = states[b, head : head + TAIL, :].astype(F32)
        reach[b : b + 1, :] = jnp.where(valid, weight, 0.0)
        weight = jnp.where(valid, weight * (tail[0:1] + tail[1:2]), weight)

    def earlier(p):
        cols = at_pair(p)
        rd = rdec[:, cols]
        total = wkv[:, cols]
        for start in range(0, n_seq, n_hid):
            left = []
            right = []
            for b in range(start, start + n_hid):
                packed = states[b, 0:head, cols].astype(F32)
                right.append(jnp.where(low_state, packed, 0.0).astype(BF16))
                right.append(jnp.where(low_state, 0.0, packed).astype(BF16))
                left.append((rd * reach[b : b + 1, cols]).astype(BF16))
            total += dot(jnp.concatenate(left, axis=1), jnp.concatenate(right, axis=0))
        wkv[:, cols] = total

    def earliers(i):
        for n in range(several):
            earlier(i * several + n)

    loop(0, pairs // several, earliers)

    def finish(p, carry):
        first, second = carry
        cols = at_pair(p)
        x = wkv[:, cols]
        c = x - head_sums(x, same_head) * (1.0 / head)
        spread = head_sums(c * c, same_head) * (1.0 / head)
        n = c * lax.rsqrt(spread + EPS_GROUP) * gscale_ref[:, cols] + goffset_ref[:, cols]
        gate = gate_ref[:, cols].astype(F32)
        m = skip_ref[:, cols].astype(F32) + n * (gate / (1.0 + jnp.exp(-gate)))
        middle[:, cols] = m
        return (
            first + jnp.sum(m, axis=1, keepdims=True),
            second + jnp.sum(m * m, axis=1, keepdims=True),
        )

    zero = jnp.zeros((rows, 1), F32)

    def finishes(i, carry):
        for n in range(several):
            carry = finish(i * several + n, carry)
        return carry

    first, second = lax.fori_loop(0, pairs // several, finishes, (zero, zero))

    lane = iota((rows, LANES), 1)
    table = jnp.where(lane == 0, first, jnp.where(lane == 1, second, 0.0))
    stats[h] = table.T[0:8]

    def send_stat(i):
        z = ring(h, i, n_hid)
        return copy(stats.at[h], stats.at[h], st_send.at[i], st_recv.at[i], s, z)

    def take_stat(i):
        z = ring(h + n_hid, -i, n_hid)
        return copy(stats.at[z], stats.at[z], st_send.at[i], st_recv.at[i], s, h)

    loop(1, n_hid, lambda i: send_stat(i).start())
    loop(1, n_hid, lambda i: take_stat(i).wait_recv())
    sums = lax.fori_loop(0, n_hid, lambda z, a: a + stats[z], jnp.zeros((8, rows), F32))
    sums = jnp.concatenate([sums, jnp.zeros((LANES - 8, rows), F32)], axis=0).T
    full_width = width * n_hid
    mean = sums[:, 0:1] / full_width
    var = sums[:, 1:2] / full_width - mean * mean
    xn = (
        (middle[...] - mean) * lax.rsqrt(var + EPS_LAYER) * nscale_ref[...] + noffset_ref[...]
    ).astype(BF16)
    edge_out[...] = xn[rows - TAIL : rows]
    to_next = copy(edge_out, edge_in, edge_send, edge_recv, ring(s, 1, n_seq), h)

    @pl.when(s < n_seq - 1)
    def _():
        to_next.start()

    @pl.when(s == 0)
    def _():
        edge_in[...] = jnp.zeros_like(edge_in)

    @pl.when(s > 0)
    def _():
        to_next.wait_recv()

    wide = xn.astype(F32)
    carried = edge_in[...].astype(F32)[TAIL - 1 : TAIL]
    prev = jnp.where(iota((rows, width), 0) == 0, carried, pltpu.roll(wide, 1, 0))
    xk[...] = (wide + (prev - wide) * blend_ref[...]).astype(BF16)

    def send_z(c, i):
        z = ring(h, i, n_hid)
        source = xk.at[pl.ds(c * half, half)]
        return copy(source, planes.at[c, h], z_send.at[c, i], z_recv.at[c, i], s, z)

    def take_z(c, i):
        z = ring(h + n_hid, -i, n_hid)
        source = xk.at[pl.ds(c * half, half)]
        return copy(source, planes.at[c, z], z_send.at[c, i], z_recv.at[c, i], s, h)

    def within(source, target, send, recv):
        def start(c, far):
            return copy(
                source.at[c, far], target.at[c, g], send.at[c, far], recv.at[c, g], far * q + j, h
            )

        def take(c, far):
            return copy(
                source.at[c, far], target.at[c, far], send.at[c, far], recv.at[c, far], s, h
            )

        return start, take

    send_a, take_a = within(planes, xa, a_send, a_recv)
    send_b, take_b = within(part_out, part_in, b_send, b_recv)
    send_d, take_d = within(down_out, down_mid, d_send, d_recv)

    for c in range(2):
        loop(1, n_hid, lambda i: send_z(c, i).start())
        planes[c, h] = xk[c * half : (c + 1) * half]

    def phase_a(c):
        def start_a(i):
            z = ring(h + n_hid, -i, n_hid)

            @pl.when(i > 0)
            def _():
                take_z(c, i).wait_recv()

            @pl.when(z != g)
            def _():
                send_a(c, z).start()

            @pl.when(z == g)
            def _():
                xa[c, g] = planes[c, z]

        loop(0, n_hid, start_a)

    tile = 256 if units % 256 == 0 else units
    lines = n_hid * half

    def tile_at(n):
        return pl.ds(pl.multiple_of(n * tile, tile), tile) if tile < units else slice(None)

    def others(body):
        loop(1, n_hid, lambda i: body(ring(g, i, n_hid)))

    def phase_b(c):
        others(lambda far: take_a(c, far).wait_recv())

        def column(n):
            cols = tile_at(n)
            total_tile = dot(xa[c, :, :, 0:depth].reshape(lines, depth), w1g[0, :, cols])
            for e in range(1, q):
                piece = xa[c, :, :, e * depth : (e + 1) * depth].reshape(lines, depth)
                total_tile += dot(piece, w1g[e, :, cols])
            part_out[c, :, :, cols] = total_tile.astype(BF16).reshape(n_hid, half, tile)

        loop(0, units // tile, column)
        others(lambda far: send_b(c, far).start())

    def send_c(c, far):
        block = hidden.at[c, g]
        return copy(block, block, c_send.at[c, far], c_recv.at[c, g], far * q + j, h)

    def take_c(c, far):
        block = hidden.at[c, far]
        return copy(block, block, c_send.at[c, far], c_recv.at[c, far], s, h)

    def phase_c(c):
        others(lambda far: take_b(c, far).wait_recv())

        def activate(n):
            cols = tile_at(n)
            pre = lax.fori_loop(
                1,
                n_hid,
                lambda i, a: a + part_in[c, ring(g, i, n_hid), :, cols].astype(F32),
                part_out[c, g, :, cols].astype(F32),
            )
            hidden[c, g, :, cols] = jnp.square(jnp.maximum(pre, 0.0)).astype(BF16)

        loop(0, units // tile, activate)
        others(lambda far: send_c(c, far).start())

    depth_tile = 256 if depth % 256 == 0 else depth

    def send_y(c, far):
        return copy(
            down_mid.at[c, far], down_in.at[c, h], y_send.at[c, far], y_recv.at[c, h], s, far
        )

    def take_y(c, z):
        return copy(down_mid.at[c, z], down_in.at[c, z], y_send.at[c, z], y_recv.at[c, z], s, h)

    def onward(c, far):
        @pl.when(far != h)
        def _():
            send_y(c, far).start()

        @pl.when(far == h)
        def _():
            down_in[c, h] = down_mid[c, far]

    def phase_d(c):
        others(lambda far: take_c(c, far).wait_recv())
        for e in range(q):
            for lo in range(0, depth, depth_tile):
                col = e * depth + lo
                piece = dot(
                    hidden[c].reshape(lines, units), w2g[e, lo : lo + depth_tile, :], ((1,), (1,))
                )
                down_out[c, :, :, col : col + depth_tile] = piece.astype(BF16).reshape(
                    n_hid, half, depth_tile
                )
        others(lambda far: send_d(c, far).start())
        down_mid[c, g] = down_out[c, g]
        onward(c, g)

    def phase_y(c):
        def step(far):
            take_d(c, far).wait_recv()
            onward(c, far)

        others(step)

    phase_a(0)
    keep1.wait()
    keep2.wait()
    for e in range(1, q):
        for c in take_weight(e):
            c.wait_recv()
    phase_b(0)
    phase_a(1)
    phase_b(1)
    phase_c(0)
    phase_c(1)
    phase_d(0)
    phase_d(1)
    phase_y(0)
    phase_y(1)

    for c in range(2):
        loop(1, n_hid, lambda i: take_y(c, ring(h, i, n_hid)).wait_recv())
        span = slice(c * half, (c + 1) * half)

        def result(p):
            cols = at_pair(p)
            down = lax.fori_loop(
                0,
                n_hid,
                lambda z, a: a + down_in[c, z, :, cols].astype(F32),
                jnp.zeros((half, LANES), F32),
            )
            out_ref[span, cols] = (middle[span, cols] + down).astype(BF16)

        loop(0, pairs, result)

    loop(1, n_hid, lambda i: send_state(i).wait_send())
    for e in range(1, q):
        loop(0, n_hid, lambda i: pass_state(e, i).wait_send())
        for c in send_weight(e):
            c.wait_send()
    loop(1, n_hid, lambda i: send_stat(i).wait_send())

    @pl.when(s < n_seq - 1)
    def _():
        to_next.wait_send()

    def end_sends(i):
        far = ring(g, i, n_hid)
        for c in range(2):
            send_z(c, i).wait_send()
            for send in (send_a, send_b, send_c, send_d):
                send(c, far).wait_send()
            send_y(c, ring(h, i, n_hid)).wait_send()

    loop(1, n_hid, end_sends)


def local(n_seq, n_hid, *args):
    skip = args[0]
    boost = args[6]
    w1 = args[12]
    rows, width = skip.shape
    heads, head = boost.shape
    depth, units = w1.shape
    q = n_seq // n_hid
    vmem = pl.BlockSpec(memory_space=pltpu.VMEM)
    anywhere = pl.BlockSpec(memory_space=pl.ANY)
    dma = pltpu.SemaphoreType.DMA
    operands = list(args[:6]) + [a.reshape(1, width) for a in args[6:12]] + list(args[12:])
    return pl.pallas_call(
        functools.partial(block_kernel, n_seq, n_hid, head),
        out_shape=jax.ShapeDtypeStruct((rows, width), BF16),
        in_specs=[anywhere] * 14,
        out_specs=vmem,
        scratch_shapes=[pltpu.VMEM(a.shape, a.dtype) for a in operands[:12]]
        + [
            dma((12,)),
            pltpu.VMEM((n_seq, head + TAIL, width), BF16),
            pltpu.VMEM((rows, width), F32),
            pltpu.VMEM((rows, width), F32),
            pltpu.VMEM((rows, width), F32),
            pltpu.VMEM((rows, width), BF16),
            pltpu.VMEM((rows, width), BF16),
            pltpu.VMEM((rows, width), F32),
            pltpu.VMEM((n_hid, 8, rows), F32),
            pltpu.VMEM((TAIL, width), BF16),
            pltpu.VMEM((TAIL, width), BF16),
            pltpu.VMEM((n_seq, width), F32),
            pltpu.VMEM((rows, width), BF16),
            pltpu.VMEM((2, n_hid, rows // 2, width), BF16),
            pltpu.VMEM((2, n_hid, rows // 2, width), BF16),
            pltpu.VMEM((q, depth, units), BF16),
            pltpu.VMEM((q, depth, units), BF16),
            pltpu.VMEM((2, n_hid, rows // 2, units), BF16),
            pltpu.VMEM((2, n_hid, rows // 2, units), BF16),
            pltpu.VMEM((2, n_hid, rows // 2, units), BF16),
            pltpu.VMEM((2, n_hid, rows // 2, width), BF16),
            pltpu.VMEM((2, n_hid, rows // 2, width), BF16),
            pltpu.VMEM((2, n_hid, rows // 2, width), BF16),
            dma((n_hid,)),
            dma((n_hid,)),
            dma((q * n_hid,)),
            dma((q * n_hid,)),
            dma((n_hid,)),
            dma((n_hid,)),
            dma,
            dma,
            dma((2, q)),
            dma((2, q)),
            dma((2,)),
            dma((2, n_hid)),
            dma((2, n_hid)),
            dma((2, n_hid)),
            dma((2, n_hid)),
            dma((2, n_hid)),
            dma((2, n_hid)),
            dma((2, n_hid)),
            dma((2, n_hid)),
            dma((2, n_hid)),
            dma((2, n_hid)),
            dma((2, n_hid)),
            dma((2, n_hid)),
        ],
        compiler_params=pltpu.CompilerParams(
            collective_id=0, has_side_effects=True, vmem_limit_bytes=60 * 2**20
        ),
    )(*operands)


def solution(mesh):
    return jax.shard_map(
        functools.partial(local, mesh.shape["seq"], mesh.shape["hid"]),
        mesh=mesh,
        in_specs=(P("seq", "hid"),) * 6
        + (P("hid", None),)
        + (P("hid"),) * 5
        + (P("seq", "hid"),) * 2,
        out_specs=P("seq", "hid"),
        check_vma=False,
    )
```

```python
import functools

import jax
import jax.numpy as jnp
from jax import lax
from jax.experimental import pallas as pl
from jax.experimental.pallas import tpu as pltpu
from jax.sharding import PartitionSpec as P

EPS_GROUP = 0.00064
EPS_LAYER = 1e-05
F32 = jnp.float32
BF16 = jnp.bfloat16
LANES = 128
TAIL = 16


def dot(a, b, dims=((1,), (0,))):
    return lax.dot_general(a, b, (dims, ((), ())), preferred_element_type=F32)


def iota(shape, axis):
    return lax.broadcasted_iota(jnp.int32, shape, axis)


def halves(x):
    high = x.astype(BF16)
    return high, x - high.astype(F32)


def head_sums(x, same_head):
    high, rest = halves(x)
    return dot(high, same_head) + dot(rest.astype(BF16), same_head)


def block_kernel(
    n_seq,
    n_hid,
    head,
    skip_hbm,
    r_hbm,
    k_hbm,
    v_hbm,
    gate_hbm,
    logit_hbm,
    boost_hbm,
    gscale_hbm,
    goffset_hbm,
    nscale_hbm,
    noffset_hbm,
    blend_hbm,
    w1_ref,
    w2_ref,
    out_ref,
    skip_ref,
    r_ref,
    k_ref,
    v_ref,
    gate_ref,
    logit_ref,
    boost_ref,
    gscale_ref,
    goffset_ref,
    nscale_ref,
    noffset_ref,
    blend_ref,
    in_sems,
    states,
    wkv,
    rdec,
    rmid,
    kmid,
    kend,
    middle,
    stats,
    edge_out,
    edge_in,
    reach,
    xk,
    planes,
    xa,
    w1g,
    w2g,
    part_out,
    part_in,
    hidden,
    down_out,
    down_mid,
    down_in,
    sa_send,
    sa_recv,
    sb_send,
    sb_recv,
    st_send,
    st_recv,
    edge_send,
    edge_recv,
    w_send,
    w_recv,
    w_local,
    z_send,
    z_recv,
    a_send,
    a_recv,
    b_send,
    b_recv,
    c_send,
    c_recv,
    d_send,
    d_recv,
    y_send,
    y_recv,
):
    rows, width = skip_ref.shape
    depth, units = w1_ref.shape
    q = n_seq // n_hid
    pairs = width // LANES
    half = rows // 2
    s = lax.axis_index("seq")
    h = lax.axis_index("hid")
    g = lax.div(s, q)
    j = lax.rem(s, q)

    def at(seq, hid):
        return {"seq": seq, "hid": hid}

    def copy(src, dst, send, recv, seq, hid):
        return pltpu.make_async_remote_copy(
            src_ref=src,
            dst_ref=dst,
            send_sem=send,
            recv_sem=recv,
            device_id=at(seq, hid),
            device_id_type=pl.DeviceIdType.MESH,
        )

    def ring(base, i, size):
        return lax.rem(base + i, size)

    def loop(start, stop, body):
        def step(i, carry):
            body(i)
            return carry

        lax.fori_loop(start, stop, step, 0)

    arrivals = [
        pltpu.make_async_copy(source, target, in_sems.at[n])
        for n, (source, target) in enumerate(
            (
                (skip_hbm, skip_ref),
                (r_hbm, r_ref),
                (k_hbm, k_ref),
                (v_hbm, v_ref),
                (gate_hbm, gate_ref),
                (logit_hbm, logit_ref),
                (boost_hbm, boost_ref),
                (gscale_hbm, gscale_ref),
                (goffset_hbm, goffset_ref),
                (nscale_hbm, nscale_ref),
                (noffset_hbm, noffset_ref),
                (blend_hbm, blend_ref),
            )
        )
    ]
    for c in arrivals:
        c.start()
    keep1 = pltpu.make_async_copy(w1_ref, w1g.at[j], w_local.at[0])
    keep2 = pltpu.make_async_copy(w2_ref, w2g.at[j], w_local.at[1])
    keep1.start()
    keep2.start()

    barrier = pltpu.get_barrier_semaphore()

    def greet(seq, hid):
        pl.semaphore_signal(
            barrier, inc=1, device_id=at(seq, hid), device_id_type=pl.DeviceIdType.MESH
        )

    loop(1, n_seq, lambda i: greet(ring(s, i, n_seq), h))
    loop(1, n_hid, lambda i: greet(s, ring(h, i, n_hid)))

    for c in arrivals:
        c.wait()

    logw = -jnp.exp(logit_ref[...])
    tri = (iota((rows, rows), 0) >= iota((rows, rows), 1)).astype(F32).astype(BF16)
    top, rest = halves(logw)
    mid, rest = halves(rest)
    inclusive = dot(tri, top) + (dot(tri, mid) + dot(tri, rest.astype(BF16)))
    exclusive = inclusive - logw
    centre_row = inclusive[rows // 2 - 1 : rows // 2]
    total = inclusive[rows - 1 : rows]
    k_all = k_ref[...].astype(F32)
    kend[...] = (k_all * jnp.exp(total - inclusive)).astype(BF16)
    decay = jnp.exp(total)
    decay_high = decay.astype(BF16).astype(F32)
    tail_row = iota((TAIL, width), 0)
    states[s, head : head + TAIL, :] = jnp.where(
        tail_row == 0, decay_high, jnp.where(tail_row == 1, decay - decay_high, 0.0)
    ).astype(BF16)

    low = iota((rows, LANES), 1) < head
    low_state = iota((head, LANES), 1) < head
    strict = iota((rows, rows), 0) > iota((rows, rows), 1)
    same = (iota((LANES, LANES), 0) < head) == (iota((LANES, LANES), 1) < head)
    same_head = same.astype(F32).astype(BF16)

    def at_pair(p):
        return pl.ds(pl.multiple_of(p * LANES, LANES), LANES)

    def chunk(p):
        cols = at_pair(p)
        rm = rmid[:, cols]
        km = kmid[:, cols]
        vv = v_ref[:, cols]
        vf = vv.astype(F32)
        first = dot(jnp.where(low, rm, 0.0).astype(BF16), km, ((1,), (1,)))
        second = dot(jnp.where(low, 0.0, rm).astype(BF16), km, ((1,), (1,)))
        first = jnp.where(strict, first, 0.0).astype(BF16)
        second = jnp.where(strict, second, 0.0).astype(BF16)
        own = r_ref[:, cols].astype(F32) * boost_ref[:, cols] * k_ref[:, cols].astype(F32)
        wkv[:, cols] = (
            dot(first, jnp.where(low, vf, 0.0).astype(BF16))
            + dot(second, jnp.where(low, 0.0, vf).astype(BF16))
            + head_sums(own, same_head) * vf
        )
    def end_state(p):
        cols = at_pair(p)
        outer = dot(kend[:, cols], v_ref[:, cols], ((0,), (0,)))
        states[s, 0:head, cols] = jnp.where(
            low_state, outer[0:head], outer[head : 2 * head]
        ).astype(BF16)

    several = max(n for n in (1, 2, 4) if pairs % n == 0)

    def end_states(i):
        for n in range(several):
            end_state(i * several + n)

    def chunks(i):
        for n in range(several):
            chunk(i * several + n)

    loop(0, pairs // several, end_states)
    pl.semaphore_wait(barrier, (n_seq - 1) + (n_hid - 1))

    def send_state(i):
        peer = ring(g, i, n_hid) * q + j
        return copy(states.at[s], states.at[s], sa_send.at[i], sa_recv.at[i], peer, h)

    def recv_state(i):
        slot = ring(g + n_hid, -i, n_hid) * q + j
        return copy(states.at[slot], states.at[slot], sa_send.at[i], sa_recv.at[i], s, h)

    def pass_state(e, i):
        slot = ring(g + n_hid, -i, n_hid) * q + j
        peer = g * q + ring(j, e, q)
        n = (e - 1) * n_hid + i
        return copy(states.at[slot], states.at[slot], sb_send.at[n], sb_recv.at[n], peer, h)

    def take_state(e, i):
        slot = ring(g + n_hid, -i, n_hid) * q + ring(j + q, -e, q)
        n = (e - 1) * n_hid + i
        return copy(states.at[slot], states.at[slot], sb_send.at[n], sb_recv.at[n], s, h)

    loop(1, n_hid, lambda i: send_state(i).start())

    for e in range(1, q):
        pass_state(e, 0).start()

    r_all = r_ref[...].astype(F32)
    rdec[...] = r_all * jnp.exp(exclusive)
    rmid[...] = r_all * jnp.exp(exclusive - centre_row)
    kmid[...] = (k_all * jnp.exp(centre_row - inclusive)).astype(BF16)
    steps = pairs // several
    loop(0, steps // 2, chunks)

    def relay(i):
        recv_state(i).wait_recv()
        for e in range(1, q):
            pass_state(e, i).start()

    loop(1, n_hid, relay)

    def send_weight(e):
        peer = g * q + ring(j, e, q)
        return (
            copy(w1_ref, w1g.at[j], w_send.at[0, e], w_recv.at[0, e], peer, h),
            copy(w2_ref, w2g.at[j], w_send.at[1, e], w_recv.at[1, e], peer, h),
        )

    def take_weight(e):
        slot = ring(j + q, -e, q)
        return (
            copy(w1_ref, w1g.at[slot], w_send.at[0, e], w_recv.at[0, e], s, h),
            copy(w2_ref, w2g.at[slot], w_send.at[1, e], w_recv.at[1, e], s, h),
        )

    for e in range(1, q):
        for c in send_weight(e):
            c.start()

    loop(steps // 2, steps, chunks)
    for e in range(1, q):
        loop(0, n_hid, lambda i: take_state(e, i).wait_recv())

    weight = jnp.ones((1, width), F32)
    for b in reversed(range(n_seq)):
        valid = b < s
        tail = states[b, head : head + TAIL, :].astype(F32)
        reach[b : b + 1, :] = jnp.where(valid, weight, 0.0)
        weight = jnp.where(valid, weight * (tail[0:1] + tail[1:2]), weight)

    def earlier(p):
        cols = at_pair(p)
        rd = rdec[:, cols]
        total = wkv[:, cols]
        for start in range(0, n_seq, n_hid):
            left = []
            right = []
            for b in range(start, start + n_hid):
                packed = states[b, 0:head, cols].astype(F32)
                right.append(jnp.where(low_state, packed, 0.0).astype(BF16))
                right.append(jnp.where(low_state, 0.0, packed).astype(BF16))
                left.append((rd * reach[b : b + 1, cols]).astype(BF16))
            total += dot(jnp.concatenate(left, axis=1), jnp.concatenate(right, axis=0))
        wkv[:, cols] = total

    def earliers(i):
        for n in range(several):
            earlier(i * several + n)

    loop(0, pairs // several, earliers)

    def finish(p, carry):
        first, second = carry
        cols = at_pair(p)
        x = wkv[:, cols]
        c = x - head_sums(x, same_head) * (1.0 / head)
        spread = head_sums(c * c, same_head) * (1.0 / head)
        n = c * lax.rsqrt(spread + EPS_GROUP) * gscale_ref[:, cols] + goffset_ref[:, cols]
        gate = gate_ref[:, cols].astype(F32)
        m = skip_ref[:, cols].astype(F32) + n * (gate / (1.0 + jnp.exp(-gate)))
        middle[:, cols] = m
        return (
            first + jnp.sum(m, axis=1, keepdims=True),
            second + jnp.sum(m * m, axis=1, keepdims=True),
        )

    zero = jnp.zeros((rows, 1), F32)

    def finishes(i, carry):
        for n in range(several):
            carry = finish(i * several + n, carry)
        return carry

    first, second = lax.fori_loop(0, pairs // several, finishes, (zero, zero))

    lane = iota((rows, LANES), 1)
    table = jnp.where(lane == 0, first, jnp.where(lane == 1, second, 0.0))
    stats[h] = table.T[0:8]

    def send_stat(i):
        z = ring(h, i, n_hid)
        return copy(stats.at[h], stats.at[h], st_send.at[i], st_recv.at[i], s, z)

    def take_stat(i):
        z = ring(h + n_hid, -i, n_hid)
        return copy(stats.at[z], stats.at[z], st_send.at[i], st_recv.at[i], s, h)

    loop(1, n_hid, lambda i: send_stat(i).start())
    loop(1, n_hid, lambda i: take_stat(i).wait_recv())
    sums = lax.fori_loop(0, n_hid, lambda z, a: a + stats[z], jnp.zeros((8, rows), F32))
    sums = jnp.concatenate([sums, jnp.zeros((LANES - 8, rows), F32)], axis=0).T
    full_width = width * n_hid
    mean = sums[:, 0:1] / full_width
    var = sums[:, 1:2] / full_width - mean * mean
    xn = (
        (middle[...] - mean) * lax.rsqrt(var + EPS_LAYER) * nscale_ref[...] + noffset_ref[...]
    ).astype(BF16)
    edge_out[...] = xn[rows - TAIL : rows]
    to_next = copy(edge_out, edge_in, edge_send, edge_recv, ring(s, 1, n_seq), h)

    @pl.when(s < n_seq - 1)
    def _():
        to_next.start()

    wide = xn.astype(F32)
    prev = pltpu.roll(wide, 1, 0)
    mixed = wide + (prev - wide) * blend_ref[...]
    xk[half:rows] = mixed[half:rows].astype(BF16)

    def send_z(c, i):
        z = ring(h, i, n_hid)
        source = xk.at[pl.ds(c * half, half)]
        return copy(source, planes.at[c, h], z_send.at[c, i], z_recv.at[c, i], s, z)

    def take_z(c, i):
        z = ring(h + n_hid, -i, n_hid)
        source = xk.at[pl.ds(c * half, half)]
        return copy(source, planes.at[c, z], z_send.at[c, i], z_recv.at[c, i], s, h)

    def within(source, target, send, recv):
        def start(c, far):
            return copy(
                source.at[c, far], target.at[c, g], send.at[c, far], recv.at[c, g], far * q + j, h
            )

        def take(c, far):
            return copy(
                source.at[c, far], target.at[c, far], send.at[c, far], recv.at[c, far], s, h
            )

        return start, take

    send_a, take_a = within(planes, xa, a_send, a_recv)
    send_b, take_b = within(part_out, part_in, b_send, b_recv)
    send_d, take_d = within(down_out, down_mid, d_send, d_recv)

    def phase_z(c):
        loop(1, n_hid, lambda i: send_z(c, i).start())
        planes[c, h] = xk[c * half : (c + 1) * half]

    phase_z(1)

    @pl.when(s == 0)
    def _():
        edge_in[...] = jnp.zeros_like(edge_in)

    @pl.when(s > 0)
    def _():
        to_next.wait_recv()

    carried = edge_in[...].astype(F32)[TAIL - 1 : TAIL]
    opening = wide[0:1] + (carried - wide[0:1]) * blend_ref[...]
    xk[0:half] = jnp.where(iota((half, width), 0) == 0, opening, mixed[0:half]).astype(BF16)
    phase_z(0)

    def phase_a(c):
        def start_a(i):
            z = ring(h + n_hid, -i, n_hid)

            @pl.when(i > 0)
            def _():
                take_z(c, i).wait_recv()

            @pl.when(z != g)
            def _():
                send_a(c, z).start()

            @pl.when(z == g)
            def _():
                xa[c, g] = planes[c, z]

        loop(0, n_hid, start_a)

    tile = 256 if units % 256 == 0 else units
    lines = n_hid * half

    def tile_at(n):
        return pl.ds(pl.multiple_of(n * tile, tile), tile) if tile < units else slice(None)

    def others(body):
        loop(1, n_hid, lambda i: body(ring(g, i, n_hid)))

    def phase_b(c):
        others(lambda far: take_a(c, far).wait_recv())

        def column(n):
            cols = tile_at(n)
            total_tile = dot(xa[c, :, :, 0:depth].reshape(lines, depth), w1g[0, :, cols])
            for e in range(1, q):
                piece = xa[c, :, :, e * depth : (e + 1) * depth].reshape(lines, depth)
                total_tile += dot(piece, w1g[e, :, cols])
            part_out[c, :, :, cols] = total_tile.astype(BF16).reshape(n_hid, half, tile)

        loop(0, units // tile, column)
        others(lambda far: send_b(c, far).start())

    def send_c(c, far):
        block = hidden.at[c, g]
        return copy(block, block, c_send.at[c, far], c_recv.at[c, g], far * q + j, h)

    def take_c(c, far):
        block = hidden.at[c, far]
        return copy(block, block, c_send.at[c, far], c_recv.at[c, far], s, h)

    def phase_c(c):
        others(lambda far: take_b(c, far).wait_recv())

        def activate(n):
            cols = tile_at(n)
            pre = lax.fori_loop(
                1,
                n_hid,
                lambda i, a: a + part_in[c, ring(g, i, n_hid), :, cols].astype(F32),
                part_out[c, g, :, cols].astype(F32),
            )
            hidden[c, g, :, cols] = jnp.square(jnp.maximum(pre, 0.0)).astype(BF16)

        loop(0, units // tile, activate)
        others(lambda far: send_c(c, far).start())

    depth_tile = 256 if depth % 256 == 0 else depth

    def send_y(c, far):
        return copy(
            down_mid.at[c, far], down_in.at[c, h], y_send.at[c, far], y_recv.at[c, h], s, far
        )

    def take_y(c, z):
        return copy(down_mid.at[c, z], down_in.at[c, z], y_send.at[c, z], y_recv.at[c, z], s, h)

    def onward(c, far):
        @pl.when(far != h)
        def _():
            send_y(c, far).start()

        @pl.when(far == h)
        def _():
            down_in[c, h] = down_mid[c, far]

    def phase_d(c):
        others(lambda far: take_c(c, far).wait_recv())
        for e in range(q):
            for lo in range(0, depth, depth_tile):
                col = e * depth + lo
                piece = dot(
                    hidden[c].reshape(lines, units), w2g[e, lo : lo + depth_tile, :], ((1,), (1,))
                )
                down_out[c, :, :, col : col + depth_tile] = piece.astype(BF16).reshape(
                    n_hid, half, depth_tile
                )
        others(lambda far: send_d(c, far).start())
        down_mid[c, g] = down_out[c, g]
        onward(c, g)

    def phase_y(c):
        def step(far):
            take_d(c, far).wait_recv()
            onward(c, far)

        others(step)

    phase_a(1)
    keep1.wait()
    keep2.wait()
    for e in range(1, q):
        for c in take_weight(e):
            c.wait_recv()
    phase_b(1)
    phase_a(0)
    phase_b(0)
    phase_c(1)
    phase_c(0)
    phase_d(1)
    phase_d(0)
    phase_y(1)
    phase_y(0)

    for c in (1, 0):
        loop(1, n_hid, lambda i: take_y(c, ring(h, i, n_hid)).wait_recv())
        span = slice(c * half, (c + 1) * half)

        def result(p):
            cols = at_pair(p)
            down = lax.fori_loop(
                0,
                n_hid,
                lambda z, a: a + down_in[c, z, :, cols].astype(F32),
                jnp.zeros((half, LANES), F32),
            )
            out_ref[span, cols] = (middle[span, cols] + down).astype(BF16)

        loop(0, pairs, result)

    loop(1, n_hid, lambda i: send_state(i).wait_send())
    for e in range(1, q):
        loop(0, n_hid, lambda i: pass_state(e, i).wait_send())
        for c in send_weight(e):
            c.wait_send()
    loop(1, n_hid, lambda i: send_stat(i).wait_send())

    @pl.when(s < n_seq - 1)
    def _():
        to_next.wait_send()

    def end_sends(i):
        far = ring(g, i, n_hid)
        for c in range(2):
            send_z(c, i).wait_send()
            for send in (send_a, send_b, send_c, send_d):
                send(c, far).wait_send()
            send_y(c, ring(h, i, n_hid)).wait_send()

    loop(1, n_hid, end_sends)


def local(n_seq, n_hid, *args):
    skip = args[0]
    boost = args[6]
    w1 = args[12]
    rows, width = skip.shape
    heads, head = boost.shape
    depth, units = w1.shape
    q = n_seq // n_hid
    vmem = pl.BlockSpec(memory_space=pltpu.VMEM)
    anywhere = pl.BlockSpec(memory_space=pl.ANY)
    dma = pltpu.SemaphoreType.DMA
    operands = list(args[:6]) + [a.reshape(1, width) for a in args[6:12]] + list(args[12:])
    return pl.pallas_call(
        functools.partial(block_kernel, n_seq, n_hid, head),
        out_shape=jax.ShapeDtypeStruct((rows, width), BF16),
        in_specs=[anywhere] * 14,
        out_specs=vmem,
        scratch_shapes=[pltpu.VMEM(a.shape, a.dtype) for a in operands[:12]]
        + [
            dma((12,)),
            pltpu.VMEM((n_seq, head + TAIL, width), BF16),
            pltpu.VMEM((rows, width), F32),
            pltpu.VMEM((rows, width), F32),
            pltpu.VMEM((rows, width), F32),
            pltpu.VMEM((rows, width), BF16),
            pltpu.VMEM((rows, width), BF16),
            pltpu.VMEM((rows, width), F32),
            pltpu.VMEM((n_hid, 8, rows), F32),
            pltpu.VMEM((TAIL, width), BF16),
            pltpu.VMEM((TAIL, width), BF16),
            pltpu.VMEM((n_seq, width), F32),
            pltpu.VMEM((rows, width), BF16),
            pltpu.VMEM((2, n_hid, rows // 2, width), BF16),
            pltpu.VMEM((2, n_hid, rows // 2, width), BF16),
            pltpu.VMEM((q, depth, units), BF16),
            pltpu.VMEM((q, depth, units), BF16),
            pltpu.VMEM((2, n_hid, rows // 2, units), BF16),
            pltpu.VMEM((2, n_hid, rows // 2, units), BF16),
            pltpu.VMEM((2, n_hid, rows // 2, units), BF16),
            pltpu.VMEM((2, n_hid, rows // 2, width), BF16),
            pltpu.VMEM((2, n_hid, rows // 2, width), BF16),
            pltpu.VMEM((2, n_hid, rows // 2, width), BF16),
            dma((n_hid,)),
            dma((n_hid,)),
            dma((q * n_hid,)),
            dma((q * n_hid,)),
            dma((n_hid,)),
            dma((n_hid,)),
            dma,
            dma,
            dma((2, q)),
            dma((2, q)),
            dma((2,)),
            dma((2, n_hid)),
            dma((2, n_hid)),
            dma((2, n_hid)),
            dma((2, n_hid)),
            dma((2, n_hid)),
            dma((2, n_hid)),
            dma((2, n_hid)),
            dma((2, n_hid)),
            dma((2, n_hid)),
            dma((2, n_hid)),
            dma((2, n_hid)),
            dma((2, n_hid)),
        ],
        compiler_params=pltpu.CompilerParams(
            collective_id=0, has_side_effects=True, vmem_limit_bytes=60 * 2**20
        ),
    )(*operands)


def solution(mesh):
    return jax.shard_map(
        functools.partial(local, mesh.shape["seq"], mesh.shape["hid"]),
        mesh=mesh,
        in_specs=(P("seq", "hid"),) * 6
        + (P("hid", None),)
        + (P("hid"),) * 5
        + (P("seq", "hid"),) * 2,
        out_specs=P("seq", "hid"),
        check_vma=False,
    )
```

```python
import functools

import jax
import jax.numpy as jnp
from jax import lax
from jax.experimental import pallas as pl
from jax.experimental.pallas import tpu as pltpu
from jax.sharding import PartitionSpec as P

EPS_GROUP = 0.00064
EPS_LAYER = 1e-05
F32 = jnp.float32
BF16 = jnp.bfloat16
LANES = 128
TAIL = 16


def dot(a, b, dims=((1,), (0,))):
    return lax.dot_general(a, b, (dims, ((), ())), preferred_element_type=F32)


def iota(shape, axis):
    return lax.broadcasted_iota(jnp.int32, shape, axis)


def halves(x):
    high = x.astype(BF16)
    return high, x - high.astype(F32)


def head_sums(x, same_head):
    high, rest = halves(x)
    return dot(high, same_head) + dot(rest.astype(BF16), same_head)


def block_kernel(
    n_seq,
    n_hid,
    head,
    skip_hbm,
    r_hbm,
    k_hbm,
    v_hbm,
    gate_hbm,
    logit_hbm,
    boost_hbm,
    gscale_hbm,
    goffset_hbm,
    nscale_hbm,
    noffset_hbm,
    blend_hbm,
    w1_ref,
    w2_ref,
    out_ref,
    skip_ref,
    r_ref,
    k_ref,
    v_ref,
    gate_ref,
    logit_ref,
    boost_ref,
    gscale_ref,
    goffset_ref,
    nscale_ref,
    noffset_ref,
    blend_ref,
    in_sems,
    states,
    wkv,
    rdec,
    rmid,
    kmid,
    kend,
    middle,
    stats,
    edge_out,
    edge_in,
    reach,
    xk,
    planes,
    xa,
    w1g,
    w2g,
    part_out,
    part_in,
    hidden,
    down_out,
    down_mid,
    down_in,
    sa_send,
    sa_recv,
    sb_send,
    sb_recv,
    st_send,
    st_recv,
    edge_send,
    edge_recv,
    w_send,
    w_recv,
    w_local,
    z_send,
    z_recv,
    a_send,
    a_recv,
    b_send,
    b_recv,
    c_send,
    c_recv,
    d_send,
    d_recv,
    y_send,
    y_recv,
):
    rows, width = skip_ref.shape
    depth, units = w1_ref.shape
    q = n_seq // n_hid
    pairs = width // LANES
    half = rows // 4
    s = lax.axis_index("seq")
    h = lax.axis_index("hid")
    g = lax.div(s, q)
    j = lax.rem(s, q)

    def at(seq, hid):
        return {"seq": seq, "hid": hid}

    def copy(src, dst, send, recv, seq, hid):
        return pltpu.make_async_remote_copy(
            src_ref=src,
            dst_ref=dst,
            send_sem=send,
            recv_sem=recv,
            device_id=at(seq, hid),
            device_id_type=pl.DeviceIdType.MESH,
        )

    def ring(base, i, size):
        return lax.rem(base + i, size)

    def loop(start, stop, body):
        def step(i, carry):
            body(i)
            return carry

        lax.fori_loop(start, stop, step, 0)

    arrivals = [
        pltpu.make_async_copy(source, target, in_sems.at[n])
        for n, (source, target) in enumerate(
            (
                (skip_hbm, skip_ref),
                (r_hbm, r_ref),
                (k_hbm, k_ref),
                (v_hbm, v_ref),
                (gate_hbm, gate_ref),
                (logit_hbm, logit_ref),
                (boost_hbm, boost_ref),
                (gscale_hbm, gscale_ref),
                (goffset_hbm, goffset_ref),
                (nscale_hbm, nscale_ref),
                (noffset_hbm, noffset_ref),
                (blend_hbm, blend_ref),
            )
        )
    ]
    for c in arrivals:
        c.start()
    keep1 = pltpu.make_async_copy(w1_ref, w1g.at[j], w_local.at[0])
    keep2 = pltpu.make_async_copy(w2_ref, w2g.at[j], w_local.at[1])
    keep1.start()
    keep2.start()

    barrier = pltpu.get_barrier_semaphore()

    def greet(seq, hid):
        pl.semaphore_signal(
            barrier, inc=1, device_id=at(seq, hid), device_id_type=pl.DeviceIdType.MESH
        )

    loop(1, n_seq, lambda i: greet(ring(s, i, n_seq), h))
    loop(1, n_hid, lambda i: greet(s, ring(h, i, n_hid)))

    for c in arrivals:
        c.wait()

    logw = -jnp.exp(logit_ref[...])
    tri = (iota((rows, rows), 0) >= iota((rows, rows), 1)).astype(F32).astype(BF16)
    top, rest = halves(logw)
    mid, rest = halves(rest)
    inclusive = dot(tri, top) + (dot(tri, mid) + dot(tri, rest.astype(BF16)))
    exclusive = inclusive - logw
    centre_row = inclusive[rows // 2 - 1 : rows // 2]
    total = inclusive[rows - 1 : rows]
    k_all = k_ref[...].astype(F32)
    kend[...] = (k_all * jnp.exp(total - inclusive)).astype(BF16)
    decay = jnp.exp(total)
    decay_high = decay.astype(BF16).astype(F32)
    tail_row = iota((TAIL, width), 0)
    states[s, head : head + TAIL, :] = jnp.where(
        tail_row == 0, decay_high, jnp.where(tail_row == 1, decay - decay_high, 0.0)
    ).astype(BF16)

    low = iota((rows, LANES), 1) < head
    low_state = iota((head, LANES), 1) < head
    strict = iota((rows, rows), 0) > iota((rows, rows), 1)
    same = (iota((LANES, LANES), 0) < head) == (iota((LANES, LANES), 1) < head)
    same_head = same.astype(F32).astype(BF16)

    def at_pair(p):
        return pl.ds(pl.multiple_of(p * LANES, LANES), LANES)

    def chunk(p):
        cols = at_pair(p)
        rm = rmid[:, cols]
        km = kmid[:, cols]
        vv = v_ref[:, cols]
        vf = vv.astype(F32)
        first = dot(jnp.where(low, rm, 0.0).astype(BF16), km, ((1,), (1,)))
        second = dot(jnp.where(low, 0.0, rm).astype(BF16), km, ((1,), (1,)))
        first = jnp.where(strict, first, 0.0).astype(BF16)
        second = jnp.where(strict, second, 0.0).astype(BF16)
        own = r_ref[:, cols].astype(F32) * boost_ref[:, cols] * k_ref[:, cols].astype(F32)
        wkv[:, cols] = (
            dot(first, jnp.where(low, vf, 0.0).astype(BF16))
            + dot(second, jnp.where(low, 0.0, vf).astype(BF16))
            + head_sums(own, same_head) * vf
        )
    def end_state(p):
        cols = at_pair(p)
        outer = dot(kend[:, cols], v_ref[:, cols], ((0,), (0,)))
        states[s, 0:head, cols] = jnp.where(
            low_state, outer[0:head], outer[head : 2 * head]
        ).astype(BF16)

    several = max(n for n in (1, 2, 4) if pairs % n == 0)

    def end_states(i):
        for n in range(several):
            end_state(i * several + n)

    def chunks(i):
        for n in range(several):
            chunk(i * several + n)

    loop(0, pairs // several, end_states)
    pl.semaphore_wait(barrier, (n_seq - 1) + (n_hid - 1))

    def send_state(i):
        peer = ring(g, i, n_hid) * q + j
        return copy(states.at[s], states.at[s], sa_send.at[i], sa_recv.at[i], peer, h)

    def recv_state(i):
        slot = ring(g + n_hid, -i, n_hid) * q + j
        return copy(states.at[slot], states.at[slot], sa_send.at[i], sa_recv.at[i], s, h)

    def pass_state(e, i):
        slot = ring(g + n_hid, -i, n_hid) * q + j
        peer = g * q + ring(j, e, q)
        n = (e - 1) * n_hid + i
        return copy(states.at[slot], states.at[slot], sb_send.at[n], sb_recv.at[n], peer, h)

    def take_state(e, i):
        slot = ring(g + n_hid, -i, n_hid) * q + ring(j + q, -e, q)
        n = (e - 1) * n_hid + i
        return copy(states.at[slot], states.at[slot], sb_send.at[n], sb_recv.at[n], s, h)

    loop(1, n_hid, lambda i: send_state(i).start())

    for e in range(1, q):
        pass_state(e, 0).start()

    r_all = r_ref[...].astype(F32)
    rdec[...] = r_all * jnp.exp(exclusive)
    rmid[...] = r_all * jnp.exp(exclusive - centre_row)
    kmid[...] = (k_all * jnp.exp(centre_row - inclusive)).astype(BF16)
    steps = pairs // several
    loop(0, steps // 2, chunks)

    def relay(i):
        recv_state(i).wait_recv()
        for e in range(1, q):
            pass_state(e, i).start()

    loop(1, n_hid, relay)

    def send_weight(e):
        peer = g * q + ring(j, e, q)
        return (
            copy(w1_ref, w1g.at[j], w_send.at[0, e], w_recv.at[0, e], peer, h),
            copy(w2_ref, w2g.at[j], w_send.at[1, e], w_recv.at[1, e], peer, h),
        )

    def take_weight(e):
        slot = ring(j + q, -e, q)
        return (
            copy(w1_ref, w1g.at[slot], w_send.at[0, e], w_recv.at[0, e], s, h),
            copy(w2_ref, w2g.at[slot], w_send.at[1, e], w_recv.at[1, e], s, h),
        )

    for e in range(1, q):
        for c in send_weight(e):
            c.start()

    loop(steps // 2, steps, chunks)
    for e in range(1, q):
        loop(0, n_hid, lambda i: take_state(e, i).wait_recv())

    weight = jnp.ones((1, width), F32)
    for b in reversed(range(n_seq)):
        valid = b < s
        tail = states[b, head : head + TAIL, :].astype(F32)
        reach[b : b + 1, :] = jnp.where(valid, weight, 0.0)
        weight = jnp.where(valid, weight * (tail[0:1] + tail[1:2]), weight)

    def earlier(p):
        cols = at_pair(p)
        rd = rdec[:, cols]
        total = wkv[:, cols]
        for start in range(0, n_seq, n_hid):
            left = []
            right = []
            for b in range(start, start + n_hid):
                packed = states[b, 0:head, cols].astype(F32)
                right.append(jnp.where(low_state, packed, 0.0).astype(BF16))
                right.append(jnp.where(low_state, 0.0, packed).astype(BF16))
                left.append((rd * reach[b : b + 1, cols]).astype(BF16))
            total += dot(jnp.concatenate(left, axis=1), jnp.concatenate(right, axis=0))
        wkv[:, cols] = total

    def earliers(i):
        for n in range(several):
            earlier(i * several + n)

    loop(0, pairs // several, earliers)

    def finish(p, carry):
        first, second = carry
        cols = at_pair(p)
        x = wkv[:, cols]
        c = x - head_sums(x, same_head) * (1.0 / head)
        spread = head_sums(c * c, same_head) * (1.0 / head)
        n = c * lax.rsqrt(spread + EPS_GROUP) * gscale_ref[:, cols] + goffset_ref[:, cols]
        gate = gate_ref[:, cols].astype(F32)
        m = skip_ref[:, cols].astype(F32) + n * (gate / (1.0 + jnp.exp(-gate)))
        middle[:, cols] = m
        return (
            first + jnp.sum(m, axis=1, keepdims=True),
            second + jnp.sum(m * m, axis=1, keepdims=True),
        )

    zero = jnp.zeros((rows, 1), F32)

    def finishes(i, carry):
        for n in range(several):
            carry = finish(i * several + n, carry)
        return carry

    first, second = lax.fori_loop(0, pairs // several, finishes, (zero, zero))

    lane = iota((rows, LANES), 1)
    table = jnp.where(lane == 0, first, jnp.where(lane == 1, second, 0.0))
    stats[h] = table.T[0:8]

    def send_stat(i):
        z = ring(h, i, n_hid)
        return copy(stats.at[h], stats.at[h], st_send.at[i], st_recv.at[i], s, z)

    def take_stat(i):
        z = ring(h + n_hid, -i, n_hid)
        return copy(stats.at[z], stats.at[z], st_send.at[i], st_recv.at[i], s, h)

    loop(1, n_hid, lambda i: send_stat(i).start())
    loop(1, n_hid, lambda i: take_stat(i).wait_recv())
    sums = lax.fori_loop(0, n_hid, lambda z, a: a + stats[z], jnp.zeros((8, rows), F32))
    sums = jnp.concatenate([sums, jnp.zeros((LANES - 8, rows), F32)], axis=0).T
    full_width = width * n_hid
    mean = sums[:, 0:1] / full_width
    var = sums[:, 1:2] / full_width - mean * mean
    xn = (
        (middle[...] - mean) * lax.rsqrt(var + EPS_LAYER) * nscale_ref[...] + noffset_ref[...]
    ).astype(BF16)
    edge_out[...] = xn[rows - TAIL : rows]
    to_next = copy(edge_out, edge_in, edge_send, edge_recv, ring(s, 1, n_seq), h)

    @pl.when(s < n_seq - 1)
    def _():
        to_next.start()

    wide = xn.astype(F32)
    prev = pltpu.roll(wide, 1, 0)
    mixed = wide + (prev - wide) * blend_ref[...]
    xk[half:rows] = mixed[half:rows].astype(BF16)

    def send_z(c, i):
        z = ring(h, i, n_hid)
        source = xk.at[pl.ds(c * half, half)]
        return copy(source, planes.at[c, h], z_send.at[c, i], z_recv.at[c, i], s, z)

    def take_z(c, i):
        z = ring(h + n_hid, -i, n_hid)
        source = xk.at[pl.ds(c * half, half)]
        return copy(source, planes.at[c, z], z_send.at[c, i], z_recv.at[c, i], s, h)

    def within(source, target, send, recv):
        def start(c, far):
            return copy(
                source.at[c, far], target.at[c, g], send.at[c, far], recv.at[c, g], far * q + j, h
            )

        def take(c, far):
            return copy(
                source.at[c, far], target.at[c, far], send.at[c, far], recv.at[c, far], s, h
            )

        return start, take

    send_a, take_a = within(planes, xa, a_send, a_recv)
    send_b, take_b = within(part_out, part_in, b_send, b_recv)
    send_d, take_d = within(down_out, down_mid, d_send, d_recv)

    def phase_z(c):
        loop(1, n_hid, lambda i: send_z(c, i).start())
        planes[c, h] = xk[c * half : (c + 1) * half]

    for c in range(1, 4):
        phase_z(c)

    @pl.when(s == 0)
    def _():
        edge_in[...] = jnp.zeros_like(edge_in)

    @pl.when(s > 0)
    def _():
        to_next.wait_recv()

    carried = edge_in[...].astype(F32)[TAIL - 1 : TAIL]
    opening = wide[0:1] + (carried - wide[0:1]) * blend_ref[...]
    xk[0:half] = jnp.where(iota((half, width), 0) == 0, opening, mixed[0:half]).astype(BF16)
    phase_z(0)

    def phase_a(c):
        def start_a(i):
            z = ring(h + n_hid, -i, n_hid)

            @pl.when(i > 0)
            def _():
                take_z(c, i).wait_recv()

            @pl.when(z != g)
            def _():
                send_a(c, z).start()

            @pl.when(z == g)
            def _():
                xa[c, g] = planes[c, z]

        loop(0, n_hid, start_a)

    tile = 256 if units % 256 == 0 else units
    lines = n_hid * half

    def tile_at(n):
        return pl.ds(pl.multiple_of(n * tile, tile), tile) if tile < units else slice(None)

    def others(body):
        loop(1, n_hid, lambda i: body(ring(g, i, n_hid)))

    def phase_b(c):
        others(lambda far: take_a(c, far).wait_recv())

        def column(n):
            cols = tile_at(n)
            total_tile = dot(xa[c, :, :, 0:depth].reshape(lines, depth), w1g[0, :, cols])
            for e in range(1, q):
                piece = xa[c, :, :, e * depth : (e + 1) * depth].reshape(lines, depth)
                total_tile += dot(piece, w1g[e, :, cols])
            part_out[c, :, :, cols] = total_tile.astype(BF16).reshape(n_hid, half, tile)

        loop(0, units // tile, column)
        others(lambda far: send_b(c, far).start())

    def send_c(c, far):
        block = hidden.at[c, g]
        return copy(block, block, c_send.at[c, far], c_recv.at[c, g], far * q + j, h)

    def take_c(c, far):
        block = hidden.at[c, far]
        return copy(block, block, c_send.at[c, far], c_recv.at[c, far], s, h)

    def phase_c(c):
        others(lambda far: take_b(c, far).wait_recv())

        def activate(n):
            cols = tile_at(n)
            pre = lax.fori_loop(
                1,
                n_hid,
                lambda i, a: a + part_in[c, ring(g, i, n_hid), :, cols].astype(F32),
                part_out[c, g, :, cols].astype(F32),
            )
            hidden[c, g, :, cols] = jnp.square(jnp.maximum(pre, 0.0)).astype(BF16)

        loop(0, units // tile, activate)
        others(lambda far: send_c(c, far).start())

    depth_tile = 256 if depth % 256 == 0 else depth

    def send_y(c, far):
        return copy(
            down_mid.at[c, far], down_in.at[c, h], y_send.at[c, far], y_recv.at[c, h], s, far
        )

    def take_y(c, z):
        return copy(down_mid.at[c, z], down_in.at[c, z], y_send.at[c, z], y_recv.at[c, z], s, h)

    def onward(c, far):
        @pl.when(far != h)
        def _():
            send_y(c, far).start()

        @pl.when(far == h)
        def _():
            down_in[c, h] = down_mid[c, far]

    def phase_d(c):
        others(lambda far: take_c(c, far).wait_recv())
        for e in range(q):
            for lo in range(0, depth, depth_tile):
                col = e * depth + lo
                piece = dot(
                    hidden[c].reshape(lines, units), w2g[e, lo : lo + depth_tile, :], ((1,), (1,))
                )
                down_out[c, :, :, col : col + depth_tile] = piece.astype(BF16).reshape(
                    n_hid, half, depth_tile
                )
        others(lambda far: send_d(c, far).start())
        down_mid[c, g] = down_out[c, g]
        onward(c, g)

    def phase_y(c):
        def step(far):
            take_d(c, far).wait_recv()
            onward(c, far)

        others(step)

    phase_a(1)
    keep1.wait()
    keep2.wait()
    for e in range(1, q):
        for c in take_weight(e):
            c.wait_recv()
    phase_b(1)
    for c in (2, 3, 0):
        phase_a(c)
        phase_b(c)
    for phase in (phase_c, phase_d, phase_y):
        for c in (1, 2, 3, 0):
            phase(c)

    for c in (1, 2, 3, 0):
        loop(1, n_hid, lambda i: take_y(c, ring(h, i, n_hid)).wait_recv())
        span = slice(c * half, (c + 1) * half)

        def result(p):
            cols = at_pair(p)
            down = lax.fori_loop(
                0,
                n_hid,
                lambda z, a: a + down_in[c, z, :, cols].astype(F32),
                jnp.zeros((half, LANES), F32),
            )
            out_ref[span, cols] = (middle[span, cols] + down).astype(BF16)

        loop(0, pairs, result)

    loop(1, n_hid, lambda i: send_state(i).wait_send())
    for e in range(1, q):
        loop(0, n_hid, lambda i: pass_state(e, i).wait_send())
        for c in send_weight(e):
            c.wait_send()
    loop(1, n_hid, lambda i: send_stat(i).wait_send())

    @pl.when(s < n_seq - 1)
    def _():
        to_next.wait_send()

    def end_sends(i):
        far = ring(g, i, n_hid)
        for c in range(4):
            send_z(c, i).wait_send()
            for send in (send_a, send_b, send_c, send_d):
                send(c, far).wait_send()
            send_y(c, ring(h, i, n_hid)).wait_send()

    loop(1, n_hid, end_sends)


def local(n_seq, n_hid, *args):
    skip = args[0]
    boost = args[6]
    w1 = args[12]
    rows, width = skip.shape
    heads, head = boost.shape
    depth, units = w1.shape
    q = n_seq // n_hid
    vmem = pl.BlockSpec(memory_space=pltpu.VMEM)
    anywhere = pl.BlockSpec(memory_space=pl.ANY)
    dma = pltpu.SemaphoreType.DMA
    operands = list(args[:6]) + [a.reshape(1, width) for a in args[6:12]] + list(args[12:])
    return pl.pallas_call(
        functools.partial(block_kernel, n_seq, n_hid, head),
        out_shape=jax.ShapeDtypeStruct((rows, width), BF16),
        in_specs=[anywhere] * 14,
        out_specs=vmem,
        scratch_shapes=[pltpu.VMEM(a.shape, a.dtype) for a in operands[:12]]
        + [
            dma((12,)),
            pltpu.VMEM((n_seq, head + TAIL, width), BF16),
            pltpu.VMEM((rows, width), F32),
            pltpu.VMEM((rows, width), F32),
            pltpu.VMEM((rows, width), F32),
            pltpu.VMEM((rows, width), BF16),
            pltpu.VMEM((rows, width), BF16),
            pltpu.VMEM((rows, width), F32),
            pltpu.VMEM((n_hid, 8, rows), F32),
            pltpu.VMEM((TAIL, width), BF16),
            pltpu.VMEM((TAIL, width), BF16),
            pltpu.VMEM((n_seq, width), F32),
            pltpu.VMEM((rows, width), BF16),
            pltpu.VMEM((4, n_hid, rows // 4, width), BF16),
            pltpu.VMEM((4, n_hid, rows // 4, width), BF16),
            pltpu.VMEM((q, depth, units), BF16),
            pltpu.VMEM((q, depth, units), BF16),
            pltpu.VMEM((4, n_hid, rows // 4, units), BF16),
            pltpu.VMEM((4, n_hid, rows // 4, units), BF16),
            pltpu.VMEM((4, n_hid, rows // 4, units), BF16),
            pltpu.VMEM((4, n_hid, rows // 4, width), BF16),
            pltpu.VMEM((4, n_hid, rows // 4, width), BF16),
            pltpu.VMEM((4, n_hid, rows // 4, width), BF16),
            dma((n_hid,)),
            dma((n_hid,)),
            dma((q * n_hid,)),
            dma((q * n_hid,)),
            dma((n_hid,)),
            dma((n_hid,)),
            dma,
            dma,
            dma((2, q)),
            dma((2, q)),
            dma((2,)),
            dma((4, n_hid)),
            dma((4, n_hid)),
            dma((4, n_hid)),
            dma((4, n_hid)),
            dma((4, n_hid)),
            dma((4, n_hid)),
            dma((4, n_hid)),
            dma((4, n_hid)),
            dma((4, n_hid)),
            dma((4, n_hid)),
            dma((4, n_hid)),
            dma((4, n_hid)),
        ],
        compiler_params=pltpu.CompilerParams(
            collective_id=0, has_side_effects=True, vmem_limit_bytes=60 * 2**20
        ),
    )(*operands)


def solution(mesh):
    return jax.shard_map(
        functools.partial(local, mesh.shape["seq"], mesh.shape["hid"]),
        mesh=mesh,
        in_specs=(P("seq", "hid"),) * 6
        + (P("hid", None),)
        + (P("hid"),) * 5
        + (P("seq", "hid"),) * 2,
        out_specs=P("seq", "hid"),
        check_vma=False,
    )
```
